512 devices in a mesh: gx: 4 (over z_hi, core), gy: 32 (over z_lo, x), gz: 4 (over y).
Axes of the slice: x: 4, y: 4, z: 16 (z_hi: 2, z_lo: 8; z = z_hi * 8 + z_lo), core: 2. Of those that a mesh axis runs over, the one named last changes fastest.
Arguments:
- positions: float32 [3, 16, 32, 8, 128], P(None, 'gx', 'gy', 'gz'), as said below
- occupied: int32 [16, 32, 8, 128], P('gx', 'gy', 'gz'), may hold values 0 or 1
Outputs:
- force_out: float32 [3, 16, 32, 8, 128], P(None, 'gx', 'gy', 'gz')
- energy: float32 [16, 32, 8, 128], P('gx', 'gy', 'gz')
The draws below stay inside these ranges and needn't reach their ends.
Inputs may be any that keep to these rules, and one draw needn't show every extreme that they name: `positions`: slot s of a tile is basis atom b = s % 4 of unit cell c = s // 4, with cell indices n_x = c // 16, n_y = (c // 4) % 4, n_z = c % 4; the basis offsets are (0, 0, 0), (0.5, 0.5, 0), (0.5, 0, 0.5), (0, 0.5, 0.5) for b = 0 to 3; each coordinate lies within 0.35 of (n + offset + 0.25) * 3.615.
All inputs are finite; a program needn't handle non-finite values. No bound on the sum of `occupied` on one device may be relied on, other than what follows from the above.
Results may differ from the reference program's by a relative error of at most 0.0003.
Values sent between devices are 32-bit elements; how exact they have to be, the bound alone decides.
A program may use at most 64 MiB of HBM per device.

```python
import math
import jax
import jax.numpy as jnp
from jax import lax

SX = 2
SY = 4
SZ = 4
SLOTS = 128
NX = 16
NY = 32
NZ = 8


def draw_positions(key, part):
    key = jax.random.fold_in(key, 7)
    slot_index = jnp.arange(SLOTS)
    cell_index = slot_index // 4
    basis_index = slot_index % 4
    basis_x = jnp.where((basis_index == 1) | (basis_index == 2), 0.5, 0.0)
    basis_y = jnp.where((basis_index == 1) | (basis_index == 3), 0.5, 0.0)
    basis_z = jnp.where((basis_index == 2) | (basis_index == 3), 0.5, 0.0)
    lattice = jnp.stack([(cell_index // (SY * SZ)).astype(jnp.float32) + basis_x, (cell_index // SZ % SY).astype(jnp.float32) + basis_y, (cell_index % SZ).astype(jnp.float32) + basis_z]).astype(jnp.float32)
    site_base = ((lattice + 0.25) * 3.615).reshape(3, 1, 1, 1, SLOTS)
    shape_all = (3, NX, NY, NZ, SLOTS)
    jitter = jax.random.uniform(key, shape_all, jnp.float32, -0.35, 0.35)
    return site_base + jitter


def with_ends(values, own_key, smallest, high):
    longest = values.shape.index(max(values.shape))
    spots = []
    for shift in (0, 1):
        where = [jax.random.randint(jax.random.fold_in(own_key, axis), (), 0, length) for axis, length in enumerate(values.shape)]
        where[longest] = (where[longest] + shift) % values.shape[longest]
        spots.append(tuple(where))
    return values.at[spots[0]].set(smallest).at[spots[1]].set(high)


def setup_inputs(seed: int = 0) -> dict:
    key_list = jax.random.split(jax.random.key(seed), 3)
    positions = draw_positions(jax.random.fold_in(key_list[2], 71), 0)
    occupied = with_ends((jax.random.randint(key_list[1], (NX, NY, NZ, SLOTS), 0, 50) < 49).astype(jnp.int32), jax.random.fold_in(key_list[1], 1), 0, 1)
    return {"positions": positions, "occupied": occupied}


lattice_step = 3.615
cut_radius = 4.9
decay_rate = 5.85
bond_length = 2.556
well_depth = 0.3
morse_rate = 1.36
embed_shift = 0.5
embed_quad = 0.002

def pair_terms(radius_sq):
    radius = jnp.sqrt(radius_sq)
    inside = 1.0 - radius_sq / (cut_radius * cut_radius)
    smooth = inside * inside
    smooth_slope = -4.0 * radius / (cut_radius * cut_radius) * inside
    density_raw = jnp.exp(-decay_rate * (radius / bond_length - 1.0))
    density = density_raw * smooth
    density_slope = -decay_rate / bond_length * density_raw * smooth + density_raw * smooth_slope
    nearer = jnp.exp(-morse_rate * (radius - bond_length))
    bonding = well_depth * (nearer * nearer - 2.0 * nearer)
    bonding_slope = well_depth * morse_rate * (2.0 * nearer - 2.0 * nearer * nearer)
    return (radius, density, density_slope, bonding * smooth, bonding_slope * smooth + bonding * smooth_slope)

def pair_geometry(own_tile, neighbour, offset, keep_mask):
    shift_vec = jnp.array(offset, jnp.float32).reshape((3,) + (1,) * own_tile.ndim)
    separation = neighbour[:3][..., None, :] - own_tile[:3][..., :, None] + shift_vec
    dist_sq = lax.optimization_barrier(jnp.sum(separation * separation, axis=0))
    both_live = own_tile[3][..., :, None] * neighbour[3][..., None, :]
    within = (dist_sq < cut_radius * cut_radius) & (both_live > 0.5)
    if keep_mask is not None:
        within = within & keep_mask
    safe_sq = jnp.where(within, dist_sq, 1.0)
    return (separation, safe_sq, within.astype(jnp.float32))

def density_terms(own_tile, neighbour, offset, keep_mask):
    separation, safe_sq, weight = pair_geometry(own_tile, neighbour, offset, keep_mask)
    radius, density, density_slope, bonding, bonding_slope = pair_terms(safe_sq)
    dens_w = weight * density
    bond_w = 0.5 * weight * bonding
    own_sum = jnp.stack([lax.optimization_barrier(jnp.sum(dens_w, -1)), lax.optimization_barrier(jnp.sum(bond_w, -1))])
    their_sum = jnp.stack([lax.optimization_barrier(jnp.sum(dens_w, -2)), lax.optimization_barrier(jnp.sum(bond_w, -2))])
    return (own_sum, their_sum)

def force_terms(own_tile, neighbour, slope_own, slope_their, offset, keep_mask):
    separation, safe_sq, weight = pair_geometry(own_tile, neighbour, offset, keep_mask)
    radius, density, density_slope, bonding, bonding_slope = pair_terms(safe_sq)
    coupling = weight * (bonding_slope + (slope_own[..., :, None] + slope_their[..., None, :]) * density_slope) / radius
    pulled = separation * coupling
    return (lax.optimization_barrier(jnp.sum(pulled, -1)), -lax.optimization_barrier(jnp.sum(pulled, -2)))

def embed_terms(density):
    root_term = jnp.sqrt(density + embed_shift)
    return (-root_term + embed_quad * density * density, -0.5 / root_term + 2.0 * embed_quad * density)

def to_blocks(values, block_size):
    flattened = values.reshape(values.shape[0], -1, block_size, values.shape[-1])
    return jnp.transpose(flattened, (1, 0, 2, 3))

def from_blocks(blocks, full_shape):
    return jnp.transpose(blocks, (1, 0, 2, 3)).reshape(full_shape)

def all_offsets():
    return [(step_x, step_y, step_z) for step_x in (-1, 0, 1) for step_y in (-1, 0, 1) for step_z in (-1, 0, 1)]

def reference(positions, occupied):
    size_x, size_y, size_z, slot_count = occupied.shape
    live_f = occupied.astype(jnp.float32)
    packed = jnp.concatenate([positions, live_f[None]], 0)
    widths = ((0, 0), (1, 1), (1, 1), (1, 1), (0, 0))
    padded = jnp.pad(packed, widths)
    tile_count = size_x * size_y * size_z
    block_size = math.gcd(tile_count, 256)
    own_blocks = to_blocks(packed, block_size)
    distinct = jnp.arange(slot_count)[:, None] != jnp.arange(slot_count)[None, :]
    density_sums = jnp.zeros((tile_count // block_size, 2, block_size, slot_count), jnp.float32)
    for step_x, step_y, step_z in all_offsets():
        neighbour = padded[:, 1 + step_x:1 + step_x + size_x, 1 + step_y:1 + step_y + size_y, 1 + step_z:1 + step_z + size_z]
        offset = (step_x * SX * lattice_step, step_y * SY * lattice_step, step_z * SZ * lattice_step)
        keep_mask = distinct if (step_x, step_y, step_z) == (0, 0, 0) else None

        def density_block(pair_data, offset=offset, keep_mask=keep_mask):
            return density_terms(pair_data[0], pair_data[1], offset, keep_mask)[0]
        density_sums = density_sums + lax.map(density_block, (own_blocks, to_blocks(neighbour, block_size)))
    density_sums = from_blocks(density_sums, (2, size_x, size_y, size_z, slot_count))
    embedding, slopes = embed_terms(density_sums[0])
    energy = live_f * (embedding + density_sums[1])
    slope_pad = jnp.pad(slopes[None], widths)
    slope_blocks = to_blocks(slopes[None], block_size)
    force_sums = jnp.zeros((tile_count // block_size, 3, block_size, slot_count), jnp.float32)
    for step_x, step_y, step_z in all_offsets():
        neighbour = padded[:, 1 + step_x:1 + step_x + size_x, 1 + step_y:1 + step_y + size_y, 1 + step_z:1 + step_z + size_z]
        their_slope = slope_pad[:, 1 + step_x:1 + step_x + size_x, 1 + step_y:1 + step_y + size_y, 1 + step_z:1 + step_z + size_z]
        offset = (step_x * SX * lattice_step, step_y * SY * lattice_step, step_z * SZ * lattice_step)
        keep_mask = distinct if (step_x, step_y, step_z) == (0, 0, 0) else None

        def force_block(pair_data, offset=offset, keep_mask=keep_mask):
            return force_terms(pair_data[0], pair_data[1], pair_data[2][0], pair_data[3][0], offset, keep_mask)[0]
        force_sums = force_sums + lax.map(force_block, (own_blocks, to_blocks(neighbour, block_size), slope_blocks, to_blocks(their_slope, block_size)))
    force_out = from_blocks(force_sums, (3, size_x, size_y, size_z, slot_count)) * live_f[None]
    return (force_out, energy)
```

```python
import math

import jax
import jax.numpy as jnp
from jax import lax
from jax.experimental import pallas as pl
from jax.experimental.pallas import tpu as pltpu
from jax.sharding import PartitionSpec as P

MESH = pl.DeviceIdType.MESH

lattice_step = 3.615
cut_radius = 4.9
far_away = 1000.0

TILE_X = 2 * lattice_step
TILE_YZ = 4 * lattice_step
REACH = 3


def displacements():
    found = []
    near = lambda n: max(0.0, abs(n) * 0.5 * lattice_step - 0.7) ** 2
    for a in range(-4, 5):
        for b in range(-4, 5):
            for c in range(-4, 5):
                if (a + b + c) % 2 == 0 and (a, b, c) != (0, 0, 0):
                    if near(a) + near(b) + near(c) < cut_radius * cut_radius + 0.01:
                        found.append((a, b, c))
    return found


VECTORS = displacements()
ZS = sorted({v[2] for v in VECTORS})
BY_Z = {dz: [(v[0], v[1]) for v in VECTORS if v[2] == dz] for dz in ZS}
ORDER = {v: i for i, v in enumerate([(a, b, dz) for dz in ZS for a, b in BY_Z[dz]])}

LOG2E = 1.0 / math.log(2.0)
DECAY = 5.85 / 2.556
MORSE = 1.36
K_DENS = -DECAY * cut_radius * LOG2E
DENS_SCALE = math.exp(5.85)
K_BOND = -MORSE * cut_radius * LOG2E
C_BOND = MORSE * 2.556 * LOG2E
FOUR = 4.0 / cut_radius
BOND_SCALE = 0.5 * 0.3
PULL_BOND = -0.3 * 2.0 * MORSE
PULL_DENS = -DECAY * DENS_SCALE


def iotas():
    return (
        lax.broadcasted_iota(jnp.int32, (8, 128), 0),
        lax.broadcasted_iota(jnp.int32, (8, 128), 1),
    )


def pick(x, idx, axis):
    return jnp.take_along_axis(x, idx, axis=axis, mode="promise_in_bounds")


def turn_indices():
    row, lane = iotas()
    quarter, rest = lane // 32, lane % 32
    xs, zs = rest // 8, rest % 8
    y = (quarter - row % 4 + 4) % 4
    basis = jnp.where(xs % 2 == 0, 3 * (zs % 2), 1 + zs % 2)
    first = (xs // 2) * 64 + y * 16 + (zs // 2) * 4 + basis
    second = (row // 4) * 4 + (quarter - row % 4 + 4) % 4
    third = ((rest // 8 + row) % 4) * 32 + quarter * 8 + lane % 8
    return first, second, third


def back_indices():
    row, lane = iotas()
    quarter, rest = lane // 32, lane % 32
    first = (rest // 8) * 32 + ((quarter - row % 4 + 4) % 4) * 8 + lane % 8
    second = (row // 4) * 4 + (quarter - row % 4 + 4) % 4
    basis = lane % 4
    xs = 2 * (lane // 64) + jnp.where((basis == 1) | (basis == 2), 1, 0)
    zs = 2 * ((lane // 4) % 4) + basis // 2
    third = (((lane // 16) % 4 + row) % 4) * 32 + xs * 8 + zs
    return first, second, third


def turned(x, idx):
    return pick(pick(pick(x, idx[0], 1), idx[1], 0), idx[2], 1)


def neighbours():
    return [(a, b, c) for a in (1, -1, 0) for b in (-1, 0, 1) for c in (-1, 0, 1) if (a, b, c) != (0, 0, 0)]


NEXT = neighbours()


def gather_tiles(sizes, pos_ref, occ_ref, raw_ref, occ_v, local, send, recv):
    n_x, n_y, n_z = sizes
    me_x, me_y, me_z = (lax.axis_index(a) for a in ("gx", "gy", "gz"))

    def device(a, b, c):
        return (me_x + a, lax.rem(me_y + b + n_y, n_y), lax.rem(me_z + c + n_z, n_z))

    def grouped(act):
        for a in (1, -1, 0):
            todo = [(i, v) for i, v in enumerate(NEXT) if v[0] == a]

            def run(todo=todo):
                for i, v in todo:
                    act(i, v)

            if a == 1:
                pl.when(me_x < n_x - 1)(run)
            elif a == -1:
                pl.when(me_x > 0)(run)
            else:
                run()

    barrier = pltpu.get_barrier_semaphore()
    grouped(
        lambda i, v: pl.semaphore_signal(barrier, inc=1, device_id=device(*v), device_id_type=MESH)
    )
    get_pos = pltpu.make_async_copy(pos_ref.at[:, :, 0], raw_ref.at[:, 2:6, 5:7], local.at[0])
    get_occ = pltpu.make_async_copy(occ_ref.at[:, 0], occ_v, local.at[1])
    get_pos.start()
    get_occ.start()

    def blank(where):
        def run():
            raw_ref[:, where : where + 2] = jnp.zeros((3, 2, 16, 128), jnp.float32)

        return run

    pl.when(me_x == 0)(blank(0))
    pl.when(me_x == n_x - 1)(blank(6))
    get_occ.wait()
    get_pos.wait()
    for t in range(4):
        empty = jnp.where(occ_v[t] != 0, 0.0, far_away)
        raw_ref[0, 2 + t, 5:7] = raw_ref[0, 2 + t, 5:7] + empty
    inner = jnp.where(me_x > 0, 9, 0) + jnp.where(me_x < n_x - 1, 9, 0) + 8
    pl.semaphore_wait(barrier, inner)

    def copy(i, v):
        a, b, c = v
        x_from, x_to, x_n = {0: (2, 2, 4), 1: (4, 0, 2), -1: (2, 6, 2)}[a]
        z_from, z_to, z_n = {0: (1, 1, 2), 1: (2, 0, 1), -1: (1, 3, 1)}[c]
        row = 4 * (1 - b) + z_to
        return pltpu.make_async_remote_copy(
            src_ref=raw_ref.at[:, x_from : x_from + x_n, 4 + z_from : 4 + z_from + z_n],
            dst_ref=raw_ref.at[:, x_to : x_to + x_n, row : row + z_n],
            send_sem=send.at[i],
            recv_sem=recv.at[i],
            device_id=device(a, b, c),
            device_id_type=MESH,
        )

    grouped(lambda i, v: copy(i, v).start())

    def arrived(i, v):
        copy(i, v).wait_recv()

    def arrivals():
        for a in (1, -1, 0):
            todo = [(i, v) for i, v in enumerate(NEXT) if v[0] == a]

            def run(todo=todo):
                for i, v in todo:
                    arrived(i, v)

            if a == 1:
                pl.when(me_x > 0)(run)
            elif a == -1:
                pl.when(me_x < n_x - 1)(run)
            else:
                run()

    arrivals()
    grouped(lambda i, v: copy(i, v).wait_send())


def pair_density(centre, near):
    sep = [n - c for n, c in zip(near, centre)]
    dist_sq = sep[0] * sep[0] + sep[1] * sep[1] + sep[2] * sep[2]
    inside = jnp.maximum(1.0 - dist_sq, 0.0)
    inverse = lax.rsqrt(dist_sq)
    radius = dist_sq * inverse
    part = jnp.exp2(K_DENS * radius) * inside
    return sep, inside, inverse, radius, part


def pair_all(centre, near):
    sep, inside, inverse, radius, part = pair_density(centre, near)
    nearer = jnp.exp2(K_BOND * radius + C_BOND)
    less = nearer - 2.0
    near_in = nearer * inside
    over = inside * inverse
    pull_bond = near_in * ((nearer - 1.0) * over + (FOUR / (2.0 * MORSE)) * less)
    pull_dens = part * (over + FOUR / DECAY)
    return sep, part * inside, near_in * inside * less, pull_bond, pull_dens


def forces(
    edges, raw_ref, occ_ref, force_ref, energy_ref, tiles, halves, tiles_x, halves_x, slope, slope_half, slope_x, slope_half_x, density, bond, pull, weighted,
):
    row, lane = iotas()
    low_x, high_x, low_y, high_y, low_z, high_z = edges()
    turn = turn_indices()
    third = (lane % 32) // 8
    out_z = (low_z & (third == 0)) | (high_z & (third == 3))
    far_z = jnp.where(out_z, far_away, 0.0)
    shift_z = (third - 1).astype(jnp.float32) * TILE_YZ
    odd = (lane // 32 + lane) % 2 == 1
    unit = 1.0 / cut_radius

    for t in range(8):
        for half in range(2):
            tile_y = 2 * half + row // 4
            far = far_z + jnp.where((low_y & (tile_y == 0)) | (high_y & (tile_y == 2)), far_away, 0.0)
            if t < 2:
                far = far + jnp.where(low_x, far_away, 0.0)
            if t > 5:
                far = far + jnp.where(high_x, far_away, 0.0)
            shifts = [
                far + (t - 2) * TILE_X,
                (tile_y - 1).astype(jnp.float32) * TILE_YZ,
                shift_z,
            ]
            for c in range(3):
                v = turned(raw_ref[c, t, 8 * half : 8 * half + 8], turn)
                tiles[c, t, 8 * half : 8 * half + 8] = (v + shifts[c]) * unit

    def halved(src, dst):
        dst[0:8] = src[0:8]
        dst[1:9] = jnp.where(odd, src[0:8], src[1:9])
        dst[8:16] = jnp.where(odd, src[7:15], src[8:16])

    def halved_rows(src, dst):
        flip = odd
        dst[8:16] = jnp.where(flip, src[7:15], src[8:16])
        dst[0:8] = jnp.where(flip, pltpu.roll(src[0:8], 1, 0), src[0:8])

    for c in range(3):
        for t in range(8):
            halved_rows(tiles.at[c, t], halves.at[c, t])

    quarter = lane // 32

    def moved_x(src, dst, count):
        for half in range(2):
            rows = slice(8 * half, 8 * half + 8)
            v = [src[t, rows] for t in range(count + 2)]
            for d in range(-3, 4):
                if d == 0:
                    for t in range(count):
                        dst[3, t, rows] = v[t + 1]
                    continue
                rolled = [pltpu.roll(x, (-32 * d) % 128, 1) for x in v]
                for t in range(count):
                    if d > 0:
                        dst[d + 3, t, rows] = jnp.where(quarter + d > 3, rolled[t + 2], rolled[t + 1])
                    else:
                        dst[d + 3, t, rows] = jnp.where(quarter + d < 0, rolled[t], rolled[t + 1])

    for c in range(3):
        moved_x(tiles.at[c], tiles_x.at[c], 6)
        moved_x(halves.at[c], halves_x.at[c], 6)

    def row_of(b):
        return 2 + ((b + 1) // 2 if b % 2 else b // 2)

    def near_of(t, a, b):
        source = halves_x if b % 2 else tiles_x
        r = row_of(b)
        return [source[c, a + 3, t, r : r + 8] for c in range(3)]

    def centre_of(t, dz):
        return [pltpu.roll(tiles[c, t + 1, 2:10], dz % 128, 1) for c in range(3)]

    def home(x, dz):
        return pltpu.roll(x, (-dz) % 128, 1)

    def put_slope(t, total):
        total = total * DENS_SCALE
        value = -0.5 * lax.rsqrt(total + 0.5) + 0.004 * total
        value = jnp.where(tiles[0, t + 1, 2:10] < 0.5 * far_away / cut_radius, value, 0.0)
        zeros = jnp.zeros((8, 128), jnp.float32)
        slope[t, 0:8] = zeros
        slope[t, 8:16] = zeros
        slope[t, 2:10] = value

    def outer(k, carry):
        t = 5 * k
        total = jnp.zeros((8, 128), jnp.float32)
        for dz in ZS:
            centre = centre_of(t, dz)
            here = jnp.zeros((8, 128), jnp.float32)
            for a, b in BY_Z[dz]:
                _, inside, _, _, part = pair_density(centre, near_of(t, a, b))
                here = here + part * inside
            total = total + home(here, dz)
        put_slope(t, total)
        return carry

    lax.fori_loop(0, 2, outer, 0)

    def inner(k, carry):
        t = k + 1
        totals = [jnp.zeros((8, 128), jnp.float32)] * 8
        for dz in ZS:
            centre = centre_of(t, dz)
            here = [jnp.zeros((8, 128), jnp.float32)] * 8
            for a, b in BY_Z[dz]:
                sep, dens, bonding, pull_bond, pull_dens = pair_all(centre, near_of(t, a, b))
                here[0] = here[0] + dens
                here[1] = here[1] + bonding
                for c in range(3):
                    here[2 + c] = here[2 + c] + pull_bond * sep[c]
                    w = pull_dens * sep[c]
                    here[5 + c] = here[5 + c] + w
                    weighted[c, ORDER[a, b, dz], k] = w
            totals = [x + home(y, dz) for x, y in zip(totals, here)]
        density[k] = totals[0] * DENS_SCALE
        bond[k] = totals[1] * BOND_SCALE
        for c in range(6):
            pull[c, k] = totals[2 + c]
        put_slope(t, totals[0])
        return carry

    lax.fori_loop(0, 4, inner, 0)

    for t in range(6):
        halved_rows(slope.at[t], slope_half.at[t])
    moved_x(slope, slope_x, 4)
    moved_x(slope_half, slope_half_x, 4)

    def finish(k, carry):
        totals = [jnp.zeros((8, 128), jnp.float32)] * 3
        for dz in ZS:
            here = [jnp.zeros((8, 128), jnp.float32)] * 3
            for a, b in BY_Z[dz]:
                r = row_of(b)
                s = (slope_half_x if b % 2 else slope_x)[a + 3, k, r : r + 8]
                for c in range(3):
                    here[c] = here[c] + s * weighted[c, ORDER[a, b, dz], k]
            totals = [x + home(y, dz) for x, y in zip(totals, here)]
        own = slope[k + 1, 2:10]
        for c in range(3):
            pull[c, k] = PULL_BOND * pull[c, k] + PULL_DENS * (own * pull[3 + c, k] + totals[c])
        d = density[k]
        bond[k] = bond[k] - jnp.sqrt(d + 0.5) + 0.002 * d * d
        return carry

    lax.fori_loop(0, 4, finish, 0)

    back = back_indices()

    def native(v):
        joined = [
            jnp.where(third < 2, pltpu.roll(v[2 * h], 120, 1), pltpu.roll(v[2 * h + 1], 8, 1))
            for h in range(2)
        ]
        both = jnp.where(row < 4, pltpu.roll(joined[0], 6, 0), pltpu.roll(joined[1], 2, 0))
        return turned(both, back)

    def store(dst, v):
        for t in range(4):
            dst[t, 0] = jnp.where(occ_ref[t, 0] != 0, v[2 * t : 2 * t + 2], 0.0)

    for c in range(3):
        store(force_ref.at[c], native([pull[c, k] for k in range(4)]))
    store(energy_ref, native([bond[k] for k in range(4)]))


def vmem():
    return pl.BlockSpec(memory_space=pltpu.VMEM)


def force_scratch():
    f32 = lambda *s: pltpu.VMEM(s, jnp.float32)
    return [
        f32(3, 8, 16, 128),
        f32(3, 8, 16, 128),
        f32(3, 7, 6, 16, 128),
        f32(3, 7, 6, 16, 128),
        f32(6, 16, 128),
        f32(6, 16, 128),
        f32(7, 4, 16, 128),
        f32(7, 4, 16, 128),
        f32(4, 8, 128),
        f32(4, 8, 128),
        f32(6, 4, 8, 128),
        f32(3, len(VECTORS), 4, 8, 128),
    ]


OUT = (
    jax.ShapeDtypeStruct((3, 4, 1, 2, 128), jnp.float32),
    jax.ShapeDtypeStruct((4, 1, 2, 128), jnp.float32),
)


def solution(mesh):
    sizes = tuple(mesh.shape[a] for a in ("gx", "gy", "gz"))
    n_x, n_y, n_z = sizes

    def edges():
        x, y, z = (lax.axis_index(a) for a in ("gx", "gy", "gz"))
        return x == 0, x == n_x - 1, y == 0, y == n_y - 1, z == 0, z == n_z - 1

    def step(positions, occupied):
        raw = pl.pallas_call(
            lambda *refs: gather_tiles(sizes, *refs),
            out_shape=pltpu.VMEM((3, 8, 16, 128), jnp.float32),
            in_specs=[pl.BlockSpec(memory_space=pl.ANY)] * 2,
            out_specs=vmem(),
            scratch_shapes=[
                pltpu.VMEM((4, 2, 128), jnp.int32),
                pltpu.SemaphoreType.DMA((2,)),
                pltpu.SemaphoreType.DMA((len(NEXT),)),
                pltpu.SemaphoreType.DMA((len(NEXT),)),
            ],
            compiler_params=pltpu.CompilerParams(collective_id=0, has_side_effects=True),
        )(positions, occupied)
        raw = pltpu.with_memory_space_constraint(raw, pltpu.VMEM)
        return pl.pallas_call(
            lambda *refs: forces(edges, *refs),
            out_shape=OUT,
            in_specs=[vmem(), vmem()],
            out_specs=[vmem(), vmem()],
            scratch_shapes=force_scratch(),
            compiler_params=pltpu.CompilerParams(vmem_limit_bytes=40 * 2**20),
        )(raw, occupied)

    in_specs = (P(None, "gx", "gy", "gz", None), P("gx", "gy", "gz", None))
    out_specs = (P(None, "gx", "gy", "gz", None), P("gx", "gy", "gz", None))
    return jax.shard_map(step, mesh=mesh, in_specs=in_specs, out_specs=out_specs, check_vma=False)
```

```python
import math

import jax
import jax.numpy as jnp
from jax import lax
from jax.experimental import pallas as pl
from jax.experimental.pallas import tpu as pltpu
from jax.sharding import PartitionSpec as P

MESH = pl.DeviceIdType.MESH

lattice_step = 3.615
cut_radius = 4.9
far_away = 1000.0

TILE_X = 2 * lattice_step
TILE_YZ = 4 * lattice_step
REACH = 3


def displacements():
    found = []
    near = lambda n: max(0.0, abs(n) * 0.5 * lattice_step - 0.7) ** 2
    for a in range(-4, 5):
        for b in range(-4, 5):
            for c in range(-4, 5):
                if (a + b + c) % 2 == 0 and (a, b, c) != (0, 0, 0):
                    if near(a) + near(b) + near(c) < cut_radius * cut_radius + 0.01:
                        found.append((a, b, c))
    return found


VECTORS = displacements()
ZS = sorted({v[2] for v in VECTORS})
BY_Z = {dz: [(v[0], v[1]) for v in VECTORS if v[2] == dz] for dz in ZS}
ORDER = {v: i for i, v in enumerate([(a, b, dz) for dz in ZS for a, b in BY_Z[dz]])}

LOG2E = 1.0 / math.log(2.0)
DECAY = 5.85 / 2.556
MORSE = 1.36
K_DENS = -DECAY * cut_radius * LOG2E
DENS_SCALE = math.exp(5.85)
K_BOND = -MORSE * cut_radius * LOG2E
C_BOND = MORSE * 2.556 * LOG2E
FOUR = 4.0 / cut_radius
BOND_SCALE = 0.5 * 0.3
PULL_BOND = -0.3 * 2.0 * MORSE
PULL_DENS = -DECAY * DENS_SCALE


def iotas():
    return (
        lax.broadcasted_iota(jnp.int32, (8, 128), 0),
        lax.broadcasted_iota(jnp.int32, (8, 128), 1),
    )


def pick(x, idx, axis):
    return jnp.take_along_axis(x, idx, axis=axis, mode="promise_in_bounds")


def turn_indices():
    row, lane = iotas()
    quarter, rest = lane // 32, lane % 32
    xs, zs = rest // 8, rest % 8
    y = (quarter - row % 4 + 4) % 4
    basis = jnp.where(xs % 2 == 0, 3 * (zs % 2), 1 + zs % 2)
    first = (xs // 2) * 64 + y * 16 + (zs // 2) * 4 + basis
    second = (row // 4) * 4 + (quarter - row % 4 + 4) % 4
    third = ((rest // 8 + row) % 4) * 32 + quarter * 8 + lane % 8
    return first, second, third


def back_indices():
    row, lane = iotas()
    quarter, rest = lane // 32, lane % 32
    first = (rest // 8) * 32 + ((quarter - row % 4 + 4) % 4) * 8 + lane % 8
    second = (row // 4) * 4 + (quarter - row % 4 + 4) % 4
    basis = lane % 4
    xs = 2 * (lane // 64) + jnp.where((basis == 1) | (basis == 2), 1, 0)
    zs = 2 * ((lane // 4) % 4) + basis // 2
    third = (((lane // 16) % 4 + row) % 4) * 32 + xs * 8 + zs
    return first, second, third


def turned(x, idx):
    return pick(pick(pick(x, idx[0], 1), idx[1], 0), idx[2], 1)


YZ = [(b, c) for b in (-1, 0, 1) for c in (-1, 0, 1)]
NEXT = [(a, b, c) for a in (0, 1, -1) for b, c in YZ if (a, b, c) != (0, 0, 0)]


def exchange(sizes, raw_ref, send, recv, mate_go, far_go):
    n_x, n_y, n_z = sizes
    me_x, me_y, me_z = (lax.axis_index(a) for a in ("gx", "gy", "gz"))
    inner = (me_x == 1) | (me_x == 2)
    low_pair = me_x < 2
    my_inner = jnp.where(low_pair, 1, 2)
    mate = jnp.where(low_pair, 1 - me_x, 5 - me_x)
    barrier = pltpu.get_barrier_semaphore()

    def there(b, c, sign=1):
        ok = []
        for step, me, n in ((b * sign, me_y, n_y), (c * sign, me_z, n_z)):
            if step == 1:
                ok.append(me < n - 1)
            if step == -1:
                ok.append(me > 0)
        return ok

    def when(conditions, act):
        if not conditions:
            return act()
        both = conditions[0]
        for x in conditions[1:]:
            both = both & x
        pl.when(both)(act)

    def count(steps, sign=1):
        total = 0
        for b, c in steps:
            ok = there(b, c, sign)
            if not ok:
                total = total + 1
                continue
            both = ok[0]
            for x in ok[1:]:
                both = both & x
            total = total + both.astype(jnp.int32)
        return total

    def greet(x, b, c):
        pl.semaphore_signal(
            barrier, inc=1, device_id=(x, me_y + b, me_z + c), device_id_type=MESH
        )

    around = [v for v in YZ if v != (0, 0)]

    def enter():
        far_outer = jnp.where(low_pair, 3, 0)

        def far():
            greet(mate, 0, 0)
            for b, c in YZ:
                when(there(b, c), lambda b=b, c=c: greet(far_outer, b, c))

        pl.when(inner)(far)
        pl.when(~inner)(lambda: greet(my_inner, 0, 0))
        for b, c in around:
            when(there(b, c), lambda b=b, c=c: greet(my_inner, b, c))

    def tell_mate(sem):
        pl.semaphore_signal(sem, inc=1, device_id=(mate, me_y, me_z), device_id_type=MESH)

    def copy(v):
        a, b, c = v
        i = NEXT.index(v)
        x_from, x_to, x_n = {0: (2, 2, 4), 1: (4, 0, 2), -1: (2, 6, 2)}[a]
        z_from, z_to, z_n = {0: (1, 1, 2), 1: (2, 0, 1), -1: (1, 3, 1)}[c]
        row = 4 * (1 - b) + z_to
        return pltpu.make_async_remote_copy(
            src_ref=raw_ref.at[:, x_from : x_from + x_n, 4 + z_from : 4 + z_from + z_n],
            dst_ref=raw_ref.at[:, x_to : x_to + x_n, row : row + z_n],
            send_sem=send.at[i],
            recv_sem=recv.at[i],
            device_id=(me_x + a, me_y + b, me_z + c),
            device_id_type=MESH,
        )

    def each(a, act, sign=1):
        for b, c in YZ:
            if (a, b, c) != (0, 0, 0):
                when(there(b, c, sign), lambda b=b, c=c: act(copy((a, b, c))))

    start, sent, got = (lambda x: x.start()), (lambda x: x.wait_send()), (lambda x: x.wait_recv())
    even = lax.rem(me_x, 2) == 0

    def near_all(act, sign=1):
        each(0, act, sign)
        pl.when(even == (sign == 1))(lambda: each(1, act, sign))
        pl.when(even == (sign != 1))(lambda: each(-1, act, sign))

    def far_all(act, sign=1):
        pl.when(me_x == (1 if sign == 1 else 2))(lambda: each(1, act, sign))
        pl.when(me_x == (2 if sign == 1 else 1))(lambda: each(-1, act, sign))

    def near_inner():
        pl.semaphore_wait(barrier, count(around) + count(YZ))
        tell_mate(mate_go)

    def near_outer():
        pl.semaphore_wait(mate_go, 1)

    def near():
        pl.when(inner)(near_inner)
        pl.when(~inner)(near_outer)
        near_all(start)

    def far_inner():
        pl.semaphore_wait(far_go, 1)
        far_all(start)

    def far_outer():
        pl.semaphore_wait(barrier, count(YZ) + 1)
        tell_mate(far_go)

    def far():
        pl.when(~inner)(far_outer)
        pl.when(inner)(far_inner)

    def near_got():
        near_all(got, -1)

    def far_got():
        far_all(got, -1)

    def all_sent():
        near_all(sent)
        far_all(sent)

    return enter, near, far, near_got, far_got, all_sent


def pair_density(centre, near):
    sep = [n - c for n, c in zip(near, centre)]
    dist_sq = sep[0] * sep[0] + sep[1] * sep[1] + sep[2] * sep[2]
    inside = jnp.maximum(1.0 - dist_sq, 0.0)
    inverse = lax.rsqrt(dist_sq)
    radius = dist_sq * inverse
    part = jnp.exp2(K_DENS * radius) * inside
    return sep, inside, inverse, radius, part


def pair_all(centre, near):
    sep, inside, inverse, radius, part = pair_density(centre, near)
    nearer = jnp.exp2(K_BOND * radius + C_BOND)
    less = nearer - 2.0
    near_in = nearer * inside
    over = inside * inverse
    pull_bond = near_in * ((nearer - 1.0) * over + (FOUR / (2.0 * MORSE)) * less)
    pull_dens = part * (over + FOUR / DECAY)
    return sep, part * inside, near_in * inside * less, pull_bond, pull_dens


def atoms(sizes, pos_ref, occ_ref, force_ref, energy_ref, raw, occ_v, tiles, halves, tiles_x, halves_x, slope, slope_half, slope_x, slope_half_x, density, bond, pull, weighted, local, send, recv, mate_go, far_go):
    n_x, n_y, n_z = sizes
    me_x, me_y, me_z = (lax.axis_index(a) for a in ("gx", "gy", "gz"))
    enter, near, far, near_got, far_got, all_sent = exchange(sizes, raw, send, recv, mate_go, far_go)
    enter()
    get_pos = pltpu.make_async_copy(pos_ref.at[:, :, 0], raw.at[:, 2:6, 5:7], local.at[0])
    get_occ = pltpu.make_async_copy(occ_ref.at[:, 0], occ_v, local.at[1])
    get_pos.start()
    get_occ.start()

    nothing = lambda *s: jnp.zeros(s, jnp.float32)

    def blank_x(t):
        def run():
            raw[:, t : t + 2] = nothing(3, 2, 16, 128)

        return run

    def blank_rows(rows):
        def run():
            for r in rows:
                raw[:, :, r : r + 1] = nothing(3, 8, 1, 128)

        return run

    pl.when(me_x == 0)(blank_x(0))
    pl.when(me_x == n_x - 1)(blank_x(6))
    pl.when(me_y == 0)(blank_rows((0, 1, 2, 3)))
    pl.when(me_y == n_y - 1)(blank_rows((8, 9, 10, 11)))
    pl.when(me_z == 0)(blank_rows((0, 4, 8)))
    pl.when(me_z == n_z - 1)(blank_rows((3, 7, 11)))

    get_occ.wait()
    get_pos.wait()
    for t in range(4):
        empty = jnp.where(occ_v[t] != 0, 0.0, far_away)
        raw[0, 2 + t, 5:7] = raw[0, 2 + t, 5:7] + empty

    high_pair = me_x >= 2
    waits = (me_x < 2) & (me_y < n_y // 2)
    pl.when(high_pair)(far)
    near()
    pl.when((me_x < 2) & (me_y >= n_y // 2))(far)
    near_got()

    row, lane = iotas()
    turn = turn_indices()
    third = (lane % 32) // 8
    quarter = lane // 32
    out_z = ((me_z == 0) & (third == 0)) | ((me_z == n_z - 1) & (third == 3))
    far_z = jnp.where(out_z, far_away, 0.0)
    shift_z = (third - 1).astype(jnp.float32) * TILE_YZ
    odd = (quarter + lane) % 2 == 1
    unit = 1.0 / cut_radius

    ahead = me_x < 2
    sign = jnp.where(ahead, 1, -1)

    def place(k, n):
        return jnp.where(ahead, k, n - 1 - k)

    def halved(src, dst):
        dst[8:16] = jnp.where(odd, src[7:15], src[8:16])
        dst[0:8] = jnp.where(odd, pltpu.roll(src[0:8], 1, 0), src[0:8])

    def take_tile(k, carry):
        t = place(k, 8)
        out_x = ((me_x == 0) & (t < 2)) | ((me_x == n_x - 1) & (t > 5))
        far_x = jnp.where(out_x, far_away, 0.0) + (t - 2).astype(jnp.float32) * TILE_X
        for half in range(2):
            tile_y = 2 * half + row // 4
            out_y = ((me_y == 0) & (tile_y == 0)) | ((me_y == n_y - 1) & (tile_y == 2))
            shifts = [
                far_z + jnp.where(out_y, far_away, 0.0) + far_x,
                (tile_y - 1).astype(jnp.float32) * TILE_YZ,
                shift_z,
            ]
            for c in range(3):
                v = turned(raw[c, t, 8 * half : 8 * half + 8], turn)
                tiles[c, t, 8 * half : 8 * half + 8] = (v + shifts[c]) * unit
        for c in range(3):
            halved(tiles.at[c, t], halves.at[c, t])
        return carry

    def moved_x(get, put):
        for half in range(2):
            rows = slice(8 * half, 8 * half + 8)
            v = [get(t)[rows] for t in range(3)]
            put(0)[rows] = v[1]
            for turn_by in (1, 2, 3):
                rolled = [pltpu.roll(x, 32 * turn_by, 1) for x in v]
                put(-turn_by)[rows] = jnp.where(quarter < turn_by, rolled[0], rolled[1])
                put(4 - turn_by)[rows] = jnp.where(quarter < turn_by, rolled[1], rolled[2])

    def move_tiles(k, carry):
        t = place(k, 6)
        for src, dst in ((tiles, tiles_x), (halves, halves_x)):
            for c in range(3):
                moved_x(lambda i: src.at[c, t + i], lambda d: dst.at[c, d + 3, t])
        return carry

    def move_slopes(k, carry):
        t = place(k, 6)
        for src, dst in ((slope, slope_x), (slope_half, slope_half_x)):
            moved_x(lambda i: src.at[t - 1 + i], lambda d: dst.at[d + 3, t])
        return carry

    def row_of(b):
        return 2 + ((b + 1) // 2 if b % 2 else b // 2)

    def near_of(t, a, b):
        source = halves_x if b % 2 else tiles_x
        r = row_of(b)
        return [source[c, 3 + sign * a, t, r : r + 8] for c in range(3)]

    def centre_of(t, dz):
        return [pltpu.roll(tiles[c, t + 1, 2:10], dz % 128, 1) for c in range(3)]

    def home(x, dz):
        return pltpu.roll(x, (-dz) % 128, 1)

    def put_slope(t, total):
        total = total * DENS_SCALE
        value = -0.5 * lax.rsqrt(total + 0.5) + 0.004 * total
        value = jnp.where(tiles[0, t + 1, 2:10] < 0.5 * far_away / cut_radius, value, 0.0)
        slope[t, 0:8] = nothing(8, 128)
        slope[t, 8:16] = nothing(8, 128)
        slope[t, 2:10] = value
        halved(slope.at[t], slope_half.at[t])

    def ghost_density(k):
        t = place(k, 6)
        total = nothing(8, 128)
        for dz in ZS:
            centre = centre_of(t, dz)
            here = nothing(8, 128)
            for a, b in BY_Z[dz]:
                _, inside, _, _, part = pair_density(centre, near_of(t, a, b))
                here = here + part * inside
            total = total + home(here, dz)
        put_slope(t, total)

    def own_pairs(k, wanted, add):
        t = place(k, 6)
        totals = [nothing(8, 128)] * 8
        for dz in ZS:
            centre = centre_of(t, dz)
            here = [nothing(8, 128)] * 8
            for a, b in BY_Z[dz]:
                if not wanted(a):
                    continue
                sep, dens, bonding, pull_bond, pull_dens = pair_all(centre, near_of(t, a, b))
                here[0] = here[0] + dens
                here[1] = here[1] + bonding
                for c in range(3):
                    here[2 + c] = here[2 + c] + pull_bond * sep[c]
                    w = pull_dens * sep[c]
                    here[5 + c] = here[5 + c] + w
                    weighted[c, ORDER[a, b, dz], t] = w
            totals = [x + home(y, dz) for x, y in zip(totals, here)]
        if add:
            totals = [totals[0] + density[t], totals[1] + bond[t]] + [totals[2 + c] + pull[c, t] for c in range(6)]
        density[t] = totals[0]
        bond[t] = totals[1]
        for c in range(6):
            pull[c, t] = totals[2 + c]
        return t, totals[0]

    def slope_pulls(k, wanted):
        t = place(k, 6)
        totals = [nothing(8, 128)] * 3
        for dz in ZS:
            here = [nothing(8, 128)] * 3
            for a, b in BY_Z[dz]:
                if not wanted(a):
                    continue
                r = row_of(b)
                s = (slope_half_x if b % 2 else slope_x)[3 + sign * a, t, r : r + 8]
                for c in range(3):
                    here[c] = here[c] + s * weighted[c, ORDER[a, b, dz], t]
            totals = [x + home(y, dz) for x, y in zip(totals, here)]
        for c in range(3):
            pull[3 + c, t] = pull[3 + c, t] + totals[c]

    def weigh_own(k):
        t = place(k, 6)
        own = slope[t, 2:10]
        for c in range(3):
            pull[3 + c, t] = own * pull[3 + c, t]

    every, behind, beyond = (lambda a: True), (lambda a: a <= 0), (lambda a: a > 0)

    def loop(first, last, act):
        def run(k, carry):
            act(k)
            return carry

        lax.fori_loop(first, last, run, 0)

    lax.fori_loop(0, 6, take_tile, 0)
    lax.fori_loop(0, 5, move_tiles, 0)
    ghost_density(0)

    def own_whole(k):
        t, total = own_pairs(k, every, False)
        put_slope(t, total)
        weigh_own(k)

    loop(1, 4, own_whole)
    own_pairs(4, behind, False)
    lax.fori_loop(1, 4, move_slopes, 0)
    loop(1, 3, lambda k: slope_pulls(k, every))
    slope_pulls(3, behind)

    pl.when(waits)(far)
    far_got()

    lax.fori_loop(6, 8, take_tile, 0)
    lax.fori_loop(4, 6, move_tiles, 0)
    ghost_density(5)
    t, total = own_pairs(4, beyond, True)
    put_slope(t, total)
    weigh_own(4)
    lax.fori_loop(3, 5, move_slopes, 0)
    slope_pulls(3, beyond)
    slope_pulls(4, every)

    back = back_indices()

    def native(v):
        joined = [
            jnp.where(third < 2, pltpu.roll(v[2 * h], 120, 1), pltpu.roll(v[2 * h + 1], 8, 1))
            for h in range(2)
        ]
        both = jnp.where(row < 4, pltpu.roll(joined[0], 6, 0), pltpu.roll(joined[1], 2, 0))
        return turned(both, back)

    def store(dst, v):
        for t in range(4):
            dst[t, 0] = jnp.where(occ_v[t] != 0, v[2 * t : 2 * t + 2], 0.0)

    for c in range(3):
        store(
            force_ref.at[c],
            native([PULL_BOND * pull[c, t] + PULL_DENS * pull[3 + c, t] for t in range(1, 5)]),
        )

    def energy_of(t):
        d = density[t] * DENS_SCALE
        return BOND_SCALE * bond[t] - jnp.sqrt(d + 0.5) + 0.002 * d * d

    store(energy_ref, native([energy_of(t) for t in range(1, 5)]))
    all_sent()


def put_out(force_in, energy_in, force_ref, energy_ref, sems):
    copies = [
        pltpu.make_async_copy(force_in, force_ref, sems.at[0]),
        pltpu.make_async_copy(energy_in, energy_ref, sems.at[1]),
    ]
    for x in copies:
        x.start()
    for x in copies:
        x.wait()


def scratch():
    f32 = lambda *s: pltpu.VMEM(s, jnp.float32)
    return [
        f32(3, 8, 16, 128),
        pltpu.VMEM((4, 2, 128), jnp.int32),
        f32(3, 8, 16, 128),
        f32(3, 8, 16, 128),
        f32(3, 7, 6, 16, 128),
        f32(3, 7, 6, 16, 128),
        f32(6, 16, 128),
        f32(6, 16, 128),
        f32(7, 6, 16, 128),
        f32(7, 6, 16, 128),
        f32(6, 8, 128),
        f32(6, 8, 128),
        f32(6, 6, 8, 128),
        f32(3, len(VECTORS), 6, 8, 128),
        pltpu.SemaphoreType.DMA((2,)),
        pltpu.SemaphoreType.DMA((len(NEXT),)),
        pltpu.SemaphoreType.DMA((len(NEXT),)),
        pltpu.SemaphoreType.REGULAR,
        pltpu.SemaphoreType.REGULAR,
    ]


def solution(mesh):
    sizes = tuple(mesh.shape[a] for a in ("gx", "gy", "gz"))

    def step(positions, occupied):
        positions, occupied = (pltpu.with_memory_space_constraint(x, pltpu.HBM) for x in (positions, occupied))
        found = pl.pallas_call(
            lambda *refs: atoms(sizes, *refs),
            out_shape=(pltpu.VMEM((3, 4, 1, 2, 128), jnp.float32), pltpu.VMEM((4, 1, 2, 128), jnp.float32)),
            in_specs=[pl.BlockSpec(memory_space=pl.ANY)] * 2,
            out_specs=[pl.BlockSpec(memory_space=pltpu.VMEM)] * 2,
            scratch_shapes=scratch(),
            compiler_params=pltpu.CompilerParams(
                collective_id=0, has_side_effects=True, vmem_limit_bytes=40 * 2**20
            ),
        )(positions, occupied)
        found = [pltpu.with_memory_space_constraint(x, pltpu.VMEM) for x in found]
        return pl.pallas_call(
            put_out,
            out_shape=[jax.ShapeDtypeStruct(x.shape, x.dtype) for x in found],
            in_specs=[pl.BlockSpec(memory_space=pltpu.VMEM)] * 2,
            out_specs=[pl.BlockSpec(memory_space=pl.ANY)] * 2,
            scratch_shapes=[pltpu.SemaphoreType.DMA((2,))],
        )(*found)

    in_specs = (P(None, "gx", "gy", "gz", None), P("gx", "gy", "gz", None))
    out_specs = (P(None, "gx", "gy", "gz", None), P("gx", "gy", "gz", None))
    return jax.shard_map(step, mesh=mesh, in_specs=in_specs, out_specs=out_specs, check_vma=False)
```

```python
import math

import jax
import jax.numpy as jnp
from jax import lax
from jax.experimental import pallas as pl
from jax.experimental.pallas import tpu as pltpu
from jax.sharding import PartitionSpec as P

MESH = pl.DeviceIdType.MESH

lattice_step = 3.615
cut_radius = 4.9
far_away = 1000.0

TILE_X = 2 * lattice_step
TILE_YZ = 4 * lattice_step
REACH = 3


def displacements():
    found = []
    near = lambda n: max(0.0, abs(n) * 0.5 * lattice_step - 0.7) ** 2
    for a in range(-4, 5):
        for b in range(-4, 5):
            for c in range(-4, 5):
                if (a + b + c) % 2 == 0 and (a, b, c) != (0, 0, 0):
                    if near(a) + near(b) + near(c) < cut_radius * cut_radius + 0.01:
                        found.append((a, b, c))
    return found


VECTORS = displacements()
ZS = sorted({v[2] for v in VECTORS})
BY_Z = {dz: [(v[0], v[1]) for v in VECTORS if v[2] == dz] for dz in ZS}
ORDER = {v: i for i, v in enumerate([(a, b, dz) for dz in ZS for a, b in BY_Z[dz]])}

LOG2E = 1.0 / math.log(2.0)
DECAY = 5.85 / 2.556
MORSE = 1.36
K_DENS = -DECAY * cut_radius * LOG2E
DENS_SCALE = math.exp(5.85)
K_BOND = -MORSE * cut_radius * LOG2E
C_BOND = MORSE * 2.556 * LOG2E
FOUR = 4.0 / cut_radius
BOND_SCALE = 0.5 * 0.3
PULL_BOND = -0.3 * 2.0 * MORSE
PULL_DENS = -DECAY * DENS_SCALE


def iotas():
    return (
        lax.broadcasted_iota(jnp.int32, (8, 128), 0),
        lax.broadcasted_iota(jnp.int32, (8, 128), 1),
    )


def pick(x, idx, axis):
    return jnp.take_along_axis(x, idx, axis=axis, mode="promise_in_bounds")


def turn_indices():
    row, lane = iotas()
    quarter, rest = lane // 32, lane % 32
    xs, zs = rest // 8, rest % 8
    y = (quarter - row % 4 + 4) % 4
    basis = jnp.where(xs % 2 == 0, 3 * (zs % 2), 1 + zs % 2)
    first = (xs // 2) * 64 + y * 16 + (zs // 2) * 4 + basis
    second = (row // 4) * 4 + (quarter - row % 4 + 4) % 4
    third = ((rest // 8 + row) % 4) * 32 + quarter * 8 + lane % 8
    return first, second, third


def back_indices():
    row, lane = iotas()
    quarter, rest = lane // 32, lane % 32
    part = (quarter - row + 10) % 4
    first = (rest // 8) * 32 + (part % 2 + 1) * 8 + lane % 8
    second = 2 + (quarter - row % 4 + 4) % 4
    basis = lane % 4
    xs = 2 * (lane // 64) + jnp.where((basis == 1) | (basis == 2), 1, 0)
    zs = 2 * ((lane // 4) % 4) + basis // 2
    third = (((lane // 16) % 4 + row) % 4) * 32 + xs * 8 + zs
    return part < 2, first, second, third


def turned(x, idx):
    return pick(pick(pick(x, idx[0], 1), idx[1], 0), idx[2], 1)


YZ = sorted(((b, c) for b in (-1, 0, 1) for c in (-1, 0, 1)), key=lambda v: -abs(v[0]) - abs(v[1]))
NEXT = [(a, b, c) for a in (0, 1, -1) for b, c in YZ if (a, b, c) != (0, 0, 0)]


def exchange(sizes, raw_ref, send, recv, near_go):
    n_x, n_y, n_z = sizes
    me_x, me_y, me_z = (lax.axis_index(a) for a in ("gx", "gy", "gz"))
    inner = (me_x == 1) | (me_x == 2)
    low_pair = me_x < 2
    my_outer = jnp.where(low_pair, 0, 3)
    mate = jnp.where(low_pair, 1 - me_x, 5 - me_x)
    barrier = pltpu.get_barrier_semaphore()

    def there(b, c, sign=1):
        ok = []
        for step, me, n in ((b * sign, me_y, n_y), (c * sign, me_z, n_z)):
            if step == 1:
                ok.append(me < n - 1)
            if step == -1:
                ok.append(me > 0)
        return ok

    def when(conditions, act):
        if not conditions:
            return act()
        both = conditions[0]
        for x in conditions[1:]:
            both = both & x
        pl.when(both)(act)

    def count(steps):
        total = 0
        for b, c in steps:
            ok = there(b, c)
            if not ok:
                total = total + 1
                continue
            both = ok[0]
            for x in ok[1:]:
                both = both & x
            total = total + both.astype(jnp.int32)
        return total

    def greet(x, b, c):
        pl.semaphore_signal(
            barrier, inc=1, device_id=(x, me_y + b, me_z + c), device_id_type=MESH
        )

    around = [v for v in YZ if v != (0, 0)]

    def enter():
        def as_inner():
            for b, c in YZ:
                when(there(b, c), lambda b=b, c=c: greet(3 - me_x, b, c))
            greet(mate, 0, 0)

        pl.when(inner)(as_inner)
        for b, c in around:
            when(there(b, c), lambda b=b, c=c: greet(my_outer, b, c))

    def copy(v):
        a, b, c = v
        i = NEXT.index(v)
        x_from, x_to, x_n = {0: (2, 2, 4), 1: (4, 0, 2), -1: (2, 6, 2)}[a]
        z_from, z_to, z_n = {0: (1, 1, 2), 1: (2, 0, 1), -1: (1, 3, 1)}[c]
        row = 4 * (1 - b) + z_to
        return pltpu.make_async_remote_copy(
            src_ref=raw_ref.at[:, x_from : x_from + x_n, 4 + z_from : 4 + z_from + z_n],
            dst_ref=raw_ref.at[:, x_to : x_to + x_n, row : row + z_n],
            send_sem=send.at[i],
            recv_sem=recv.at[i],
            device_id=(me_x + a, me_y + b, me_z + c),
            device_id_type=MESH,
        )

    def each(a, act, sign=1):
        for b, c in YZ:
            if (a, b, c) != (0, 0, 0):
                when(there(b, c, sign), lambda b=b, c=c: act(copy((a, b, c))))

    start, sent, got = (lambda x: x.start()), (lambda x: x.wait_send()), (lambda x: x.wait_recv())
    even = lax.rem(me_x, 2) == 0

    def near_all(act, sign=1):
        each(0, act, sign)
        pl.when(even == (sign == 1))(lambda: each(1, act, sign))
        pl.when(even == (sign != 1))(lambda: each(-1, act, sign))

    def far_all(act, sign=1):
        pl.when(me_x == (1 if sign == 1 else 2))(lambda: each(1, act, sign))
        pl.when(me_x == (2 if sign == 1 else 1))(lambda: each(-1, act, sign))

    def far_inner():
        pl.semaphore_wait(barrier, count(YZ))
        far_all(start)

    def far():
        pl.when(inner)(far_inner)

    def near_outer():
        pl.semaphore_wait(barrier, count(around) + count(YZ))
        pl.semaphore_signal(near_go, inc=1, device_id=(mate, me_y, me_z), device_id_type=MESH)

    def near():
        pl.when(~inner)(near_outer)
        pl.when(inner)(lambda: pl.semaphore_wait(near_go, 1))
        near_all(start)

    def near_got():
        near_all(got, -1)

    def far_got():
        far_all(got, -1)

    def all_sent():
        near_all(sent)
        far_all(sent)

    return enter, near, far, near_got, far_got, all_sent


def pair_density(centre, near):
    sep = [n - c for n, c in zip(near, centre)]
    dist_sq = sep[0] * sep[0] + sep[1] * sep[1] + sep[2] * sep[2]
    inside = jnp.maximum(1.0 - dist_sq, 0.0)
    inverse = lax.rsqrt(dist_sq)
    radius = dist_sq * inverse
    part = jnp.exp2(K_DENS * radius) * inside
    return sep, inside, inverse, radius, part


def pair_all(centre, near):
    sep, inside, inverse, radius, part = pair_density(centre, near)
    nearer = jnp.exp2(K_BOND * radius + C_BOND)
    less = nearer - 2.0
    near_in = nearer * inside
    over = inside * inverse
    pull_bond = near_in * ((nearer - 1.0) * over + (FOUR / (2.0 * MORSE)) * less)
    pull_dens = part * (over + FOUR / DECAY)
    return sep, part * inside, near_in * inside * less, pull_bond, pull_dens


def atoms(sizes, pos_ref, occ_ref, force_ref, energy_ref, raw, occ_v, tiles, rolled, moved, centres, slope, slope_rolled, slope_moved, density, bond, pull, weighted, local, send, recv, near_go):
    n_x, n_y, n_z = sizes
    me_x, me_y, me_z = (lax.axis_index(a) for a in ("gx", "gy", "gz"))
    enter, near, far, near_got, far_got, all_sent = exchange(sizes, raw, send, recv, near_go)
    get_pos = pltpu.make_async_copy(pos_ref.at[:, :, 0], raw.at[:, 2:6, 5:7], local.at[0])
    get_occ = pltpu.make_async_copy(occ_ref.at[:, 0], occ_v, local.at[1])
    get_pos.start()
    get_occ.start()
    enter()

    nothing = lambda *s: jnp.zeros(s, jnp.float32)

    def blank_x(t):
        def run():
            raw[:, t : t + 2] = nothing(3, 2, 16, 128)

        return run

    def blank_rows(rows):
        def run():
            for r in rows:
                raw[:, :, r : r + 1] = nothing(3, 8, 1, 128)

        return run

    get_occ.wait()
    get_pos.wait()
    for t in range(4):
        empty = jnp.where(occ_v[t] != 0, 0.0, far_away)
        raw[0, 2 + t, 5:7] = raw[0, 2 + t, 5:7] + empty

    ahead = me_x < 2
    long_ahead = me_y < (5 * n_y) // 8
    pl.when(~ahead)(far)
    near()

    pl.when(me_x == 0)(blank_x(0))
    pl.when(me_x == n_x - 1)(blank_x(6))
    pl.when(me_y == 0)(blank_rows((0, 1, 2, 3)))
    pl.when(me_y == n_y - 1)(blank_rows((8, 9, 10, 11)))
    pl.when(me_z == 0)(blank_rows((0, 4, 8)))
    pl.when(me_z == n_z - 1)(blank_rows((3, 7, 11)))

    row, lane = iotas()
    turn = turn_indices()
    third = (lane % 32) // 8
    quarter = lane // 32
    out_z = ((me_z == 0) & (third == 0)) | ((me_z == n_z - 1) & (third == 3))
    far_z = jnp.where(out_z, far_away, 0.0)
    shift_z = (third - 1).astype(jnp.float32) * TILE_YZ
    odds = [(quarter + lane + a) % 2 == 1 for a in (0, 1)]
    unit = 1.0 / cut_radius

    reach = jnp.where(ahead, quarter, 3 - quarter)

    def place(k, n):
        return jnp.where(ahead, k, n - 1 - k)

    near_got()

    def take_tile(k):
        t = place(k, 8)
        out_x = ((me_x == 0) & (t < 2)) | ((me_x == n_x - 1) & (t > 5))
        far_x = jnp.where(out_x, far_away, 0.0) + (t - 2).astype(jnp.float32) * TILE_X
        for half in range(2):
            rows = slice(8 * half, 8 * half + 8)
            tile_y = 2 * half + row // 4
            out_y = ((me_y == 0) & (tile_y == 0)) | ((me_y == n_y - 1) & (tile_y == 2))
            shifts = [
                far_z + jnp.where(out_y, far_away, 0.0) + far_x,
                (tile_y - 1).astype(jnp.float32) * TILE_YZ,
                shift_z,
            ]
            for c in range(3):
                v = (turned(raw[c, t, rows], turn) + shifts[c]) * unit
                tiles[c, k, rows] = v
                roll_planes(v, lambda a: rolled.at[c, a, k, rows])

    def roll_planes(v, put):
        for m in (1, 2, 3):
            put(jnp.where(ahead, 4 - m, m))[...] = pltpu.roll(v, 32 * m, 1)

    def crossing(a):
        return reach + a > 3 if a > 0 else reach + a < 0

    def move_tile(k, shifts):
        for a in shifts:
            for c in range(3):
                for half in range(2):
                    rows = slice(8 * half, 8 * half + 8)
                    other = k + 2 if a > 0 else k
                    moved[c, a + 3, k, rows] = jnp.where(
                        crossing(a), rolled[c, a % 4, other, rows], rolled[c, a % 4, k + 1, rows]
                    )

    def roll_slope(k, value):
        slope[k, 2:10] = value
        roll_planes(value, lambda a: slope_rolled.at[a, k])

    def move_slope(k, shifts):
        for a in shifts:
            other = k + 1 if a > 0 else k - 1
            slope_moved[a + 3, k, 2:10] = jnp.where(
                crossing(a), slope_rolled[a % 4, other], slope_rolled[a % 4, k]
            )

    def rows_of(get, a, b):
        if b % 2 == 0:
            r = 2 + b // 2
            return [x[r : r + 8] for x in get]
        r = 2 + (b + 1) // 2
        return [jnp.where(odds[a % 2], x[r - 1 : r + 7], x[r : r + 8]) for x in get]

    def near_of(k, a, b):
        return rows_of([moved.at[c, a + 3, k] if a else tiles.at[c, k + 1] for c in range(3)], a, b)

    def slope_of(k, a, b):
        return rows_of([slope_moved.at[a + 3, k] if a else slope.at[k]], a, b)[0]

    def centre_of(k, dz):
        return [pltpu.roll(tiles[c, k + 1, 2:10], dz % 128, 1) if dz else tiles[c, k + 1, 2:10] for c in range(3)]

    def home(x, dz):
        return pltpu.roll(x, (-dz) % 128, 1) if dz else x

    def slope_value(k, total):
        total = total * DENS_SCALE
        value = -0.5 * lax.rsqrt(total + 0.5) + 0.004 * total
        return jnp.where(tiles[0, k + 1, 2:10] < 0.5 * far_away / cut_radius, value, 0.0)

    def ghost_density(k):
        total = nothing(8, 128)
        for dz in ZS:
            centre = centre_of(k, dz)
            here = nothing(8, 128)
            for a, b in BY_Z[dz]:
                _, inside, _, _, part = pair_density(centre, near_of(k, a, b))
                here = here + part * inside
            total = total + home(here, dz)
        return total

    def own_pairs(k, wanted, centre_at):
        totals = [nothing(8, 128)] * 8
        for dz in ZS:
            centre = centre_at(dz)
            here = [nothing(8, 128)] * 8
            for a, b in BY_Z[dz]:
                if not wanted(a):
                    continue
                sep, dens, bonding, pull_bond, pull_dens = pair_all(centre, near_of(k, a, b))
                here[0] = here[0] + dens
                here[1] = here[1] + bonding
                for c in range(3):
                    here[2 + c] = here[2 + c] + pull_bond * sep[c]
                    w = pull_dens * sep[c]
                    here[5 + c] = here[5 + c] + w
                    weighted[c, ORDER[a, b, dz], k] = w
            totals = [x + home(y, dz) for x, y in zip(totals, here)]
        return totals

    def slope_pulls(k, wanted):
        totals = [nothing(8, 128)] * 3
        for dz in ZS:
            here = [nothing(8, 128)] * 3
            for a, b in BY_Z[dz]:
                if not wanted(a):
                    continue
                s = slope_of(k, a, b)
                for c in range(3):
                    here[c] = here[c] + s * weighted[c, ORDER[a, b, dz], k]
            totals = [x + home(y, dz) for x, y in zip(totals, here)]
        return totals

    def keep(k, totals, value):
        density[k] = totals[0]
        bond[k] = totals[1]
        for c in range(3):
            pull[c, k] = PULL_BOND * totals[2 + c] + PULL_DENS * (value * totals[5 + c])

    def add_pulls(k, totals):
        for c in range(3):
            pull[c, k] = pull[c, k] + PULL_DENS * totals[c]

    every, behind, beyond = (lambda a: True), (lambda a: a <= 0), (lambda a: a > 0)
    both_ways = (-3, -2, -1, 1, 2, 3)

    def loop(first, last, act):
        def run(k, carry):
            act(k)
            return carry

        lax.fori_loop(first, last, run, 0)

    slope[...] = nothing(6, 16, 128)
    slope_moved[...] = nothing(7, 6, 16, 128)
    loop(0, 6, take_tile)
    pl.when(ahead & ~long_ahead)(far)
    loop(0, 4, lambda k: move_tile(k, both_ways))
    move_tile(4, (-3, -2, -1))
    roll_slope(0, slope_value(0, ghost_density(0)))

    def own_whole(k):
        totals = own_pairs(k, every, lambda dz: centre_of(k, dz))
        value = slope_value(k, totals[0])
        keep(k, totals, value)
        roll_slope(k, value)

    loop(1, 4, own_whole)
    loop(1, 3, lambda k: move_slope(k, both_ways))
    move_slope(3, (-3, -2, -1))
    loop(1, 3, lambda k: add_pulls(k, slope_pulls(k, every)))
    add_pulls(3, slope_pulls(3, behind))
    for i, dz in enumerate(ZS):
        v = centre_of(4, dz)
        for c in range(3):
            centres[c, i] = v[c]

    def kept(dz):
        return [centres[c, ZS.index(dz)] for c in range(3)]

    part = own_pairs(4, behind, kept)
    density[4] = part[0]
    bond[4] = part[1]
    for c in range(6):
        pull[c + 4, 4] = part[2 + c]

    pl.when(ahead & long_ahead)(far)
    far_got()

    for k in (6, 7):
        take_tile(k)
    move_tile(4, (1, 2, 3))
    totals = own_pairs(4, beyond, kept)
    totals = [totals[0] + density[4], totals[1] + bond[4]] + [totals[2 + c] + pull[c + 4, 4] for c in range(6)]
    value = slope_value(4, totals[0])
    keep(4, totals, value)
    roll_slope(4, value)
    move_tile(5, both_ways)
    roll_slope(5, slope_value(5, ghost_density(5)))
    move_slope(3, (1, 2, 3))
    move_slope(4, both_ways)
    add_pulls(3, slope_pulls(3, beyond))
    add_pulls(4, slope_pulls(4, every))

    first_part, back, back_rows, back_slots = back_indices()

    def native(at):
        v = [at(place(p, 4) + 1) for p in range(4)]
        v = [pick(x, back, 1) for x in v]
        v = [jnp.where(first_part, v[2 * h], v[2 * h + 1]) for h in range(2)]
        v = [pick(x, back_rows, 0) for x in v]
        return pick(jnp.where(row < 4, v[0], v[1]), back_slots, 1)

    def store(dst, v):
        for t in range(4):
            dst[t, 0] = jnp.where(occ_v[t] != 0, v[2 * t : 2 * t + 2], 0.0)

    for c in range(3):
        store(force_ref.at[c], native(lambda k: pull[c, k]))

    def energy_of(k):
        d = density[k] * DENS_SCALE
        return BOND_SCALE * bond[k] - jnp.sqrt(d + 0.5) + 0.002 * d * d

    store(energy_ref, native(energy_of))
    all_sent()


def put_out(force_in, energy_in, force_ref, energy_ref, sems):
    copies = [
        pltpu.make_async_copy(force_in, force_ref, sems.at[0]),
        pltpu.make_async_copy(energy_in, energy_ref, sems.at[1]),
    ]
    for x in copies:
        x.start()
    for x in copies:
        x.wait()


def scratch():
    f32 = lambda *s: pltpu.VMEM(s, jnp.float32)
    return [
        f32(3, 8, 16, 128),
        pltpu.VMEM((4, 2, 128), jnp.int32),
        f32(3, 8, 16, 128),
        f32(3, 4, 8, 16, 128),
        f32(3, 7, 6, 16, 128),
        f32(3, len(ZS), 8, 128),
        f32(6, 16, 128),
        f32(4, 6, 8, 128),
        f32(7, 6, 16, 128),
        f32(6, 8, 128),
        f32(6, 8, 128),
        f32(10, 6, 8, 128),
        f32(3, len(VECTORS), 6, 8, 128),
        pltpu.SemaphoreType.DMA((2,)),
        pltpu.SemaphoreType.DMA((len(NEXT),)),
        pltpu.SemaphoreType.DMA((len(NEXT),)),
        pltpu.SemaphoreType.REGULAR,
    ]


def solution(mesh):
    sizes = tuple(mesh.shape[a] for a in ("gx", "gy", "gz"))

    def step(positions, occupied):
        positions, occupied = (pltpu.with_memory_space_constraint(x, pltpu.HBM) for x in (positions, occupied))
        found = pl.pallas_call(
            lambda *refs: atoms(sizes, *refs),
            out_shape=(pltpu.VMEM((3, 4, 1, 2, 128), jnp.float32), pltpu.VMEM((4, 1, 2, 128), jnp.float32)),
            in_specs=[pl.BlockSpec(memory_space=pl.ANY)] * 2,
            out_specs=[pl.BlockSpec(memory_space=pltpu.VMEM)] * 2,
            scratch_shapes=scratch(),
            compiler_params=pltpu.CompilerParams(
                collective_id=0, has_side_effects=True, vmem_limit_bytes=40 * 2**20
            ),
        )(positions, occupied)
        found = [pltpu.with_memory_space_constraint(x, pltpu.VMEM) for x in found]
        return pl.pallas_call(
            put_out,
            out_shape=[jax.ShapeDtypeStruct(x.shape, x.dtype) for x in found],
            in_specs=[pl.BlockSpec(memory_space=pltpu.VMEM)] * 2,
            out_specs=[pl.BlockSpec(memory_space=pl.ANY)] * 2,
            scratch_shapes=[pltpu.SemaphoreType.DMA((2,))],
        )(*found)

    in_specs = (P(None, "gx", "gy", "gz", None), P("gx", "gy", "gz", None))
    out_specs = (P(None, "gx", "gy", "gz", None), P("gx", "gy", "gz", None))
    return jax.shard_map(step, mesh=mesh, in_specs=in_specs, out_specs=out_specs, check_vma=False)
```

```python
import math

import jax
import jax.numpy as jnp
from jax import lax
from jax.experimental import pallas as pl
from jax.experimental.pallas import tpu as pltpu
from jax.sharding import PartitionSpec as P

MESH = pl.DeviceIdType.MESH

lattice_step = 3.615
cut_radius = 4.9
far_away = 1000.0

TILE_X = 2 * lattice_step
TILE_YZ = 4 * lattice_step
REACH = 3


def displacements():
    found = []
    near = lambda n: max(0.0, abs(n) * 0.5 * lattice_step - 0.7) ** 2
    for a in range(-4, 5):
        for b in range(-4, 5):
            for c in range(-4, 5):
                if (a + b + c) % 2 == 0 and (a, b, c) != (0, 0, 0):
                    if near(a) + near(b) + near(c) < cut_radius * cut_radius + 0.01:
                        found.append((a, b, c))
    return found


VECTORS = displacements()
ZS = sorted({v[2] for v in VECTORS})
BY_Z = {dz: [(v[0], v[1]) for v in VECTORS if v[2] == dz] for dz in ZS}
ORDER = {v: i for i, v in enumerate([(a, b, dz) for dz in ZS for a, b in BY_Z[dz]])}

LOG2E = 1.0 / math.log(2.0)
DECAY = 5.85 / 2.556
MORSE = 1.36
K_DENS = -DECAY * cut_radius * LOG2E
DENS_SCALE = math.exp(5.85)
K_BOND = -MORSE * cut_radius * LOG2E
C_BOND = MORSE * 2.556 * LOG2E
FOUR = 4.0 / cut_radius
BOND_SCALE = 0.5 * 0.3
PULL_BOND = -0.3 * 2.0 * MORSE
PULL_DENS = -DECAY * DENS_SCALE


def iotas():
    return (
        lax.broadcasted_iota(jnp.int32, (8, 128), 0),
        lax.broadcasted_iota(jnp.int32, (8, 128), 1),
    )


def pick(x, idx, axis):
    return jnp.take_along_axis(x, idx, axis=axis, mode="promise_in_bounds")


def turn_indices():
    row, lane = iotas()
    quarter, rest = lane // 32, lane % 32
    xs, zs = rest // 8, rest % 8
    y = (quarter - row % 4 + 4) % 4
    basis = jnp.where(xs % 2 == 0, 3 * (zs % 2), 1 + zs % 2)
    first = (xs // 2) * 64 + y * 16 + (zs // 2) * 4 + basis
    second = (row // 4) * 4 + (quarter - row % 4 + 4) % 4
    return first, second


def back_indices():
    row, lane = iotas()
    quarter, rest = lane // 32, lane % 32
    part = (quarter - row + 10) % 4
    first = (rest // 8) * 32 + (part % 2 + 1) * 8 + lane % 8
    second = 2 + (quarter - row % 4 + 4) % 4
    basis = lane % 4
    xs = 2 * (lane // 64) + jnp.where((basis == 1) | (basis == 2), 1, 0)
    zs = 2 * ((lane // 4) % 4) + basis // 2
    third = (((lane // 16) % 4 + row) % 4) * 32 + xs * 8 + zs
    return part < 2, first, second, third


YZ = sorted(((b, c) for b in (-1, 0, 1) for c in (-1, 0, 1)), key=lambda v: -abs(v[0]) - abs(v[1]))
NEXT = [(a, b, c) for a in (0, 1, -1) for b, c in YZ if (a, b, c) != (0, 0, 0)]


def exchange(sizes, raw_ref, send, recv, near_go):
    n_x, n_y, n_z = sizes
    me_x, me_y, me_z = (lax.axis_index(a) for a in ("gx", "gy", "gz"))
    inner = (me_x == 1) | (me_x == 2)
    low_pair = me_x < 2
    my_outer = jnp.where(low_pair, 0, 3)
    mate = jnp.where(low_pair, 1 - me_x, 5 - me_x)
    barrier = pltpu.get_barrier_semaphore()

    def there(b, c, sign=1):
        ok = []
        for step, me, n in ((b * sign, me_y, n_y), (c * sign, me_z, n_z)):
            if step == 1:
                ok.append(me < n - 1)
            if step == -1:
                ok.append(me > 0)
        return ok

    def when(conditions, act):
        if not conditions:
            return act()
        both = conditions[0]
        for x in conditions[1:]:
            both = both & x
        pl.when(both)(act)

    def count(steps):
        total = 0
        for b, c in steps:
            ok = there(b, c)
            if not ok:
                total = total + 1
                continue
            both = ok[0]
            for x in ok[1:]:
                both = both & x
            total = total + both.astype(jnp.int32)
        return total

    def greet(x, b, c):
        pl.semaphore_signal(
            barrier, inc=1, device_id=(x, me_y + b, me_z + c), device_id_type=MESH
        )

    around = [v for v in YZ if v != (0, 0)]

    def enter():
        def as_inner():
            for b, c in YZ:
                when(there(b, c), lambda b=b, c=c: greet(3 - me_x, b, c))
            greet(mate, 0, 0)

        pl.when(inner)(as_inner)
        for b, c in around:
            when(there(b, c), lambda b=b, c=c: greet(my_outer, b, c))

    def copy(v):
        a, b, c = v
        i = NEXT.index(v)
        x_from, x_to, x_n = {0: (2, 2, 4), 1: (4, 0, 2), -1: (2, 6, 2)}[a]
        z_from, z_to, z_n = {0: (1, 1, 2), 1: (2, 0, 1), -1: (1, 3, 1)}[c]
        row = 4 * (1 - b) + z_to
        return pltpu.make_async_remote_copy(
            src_ref=raw_ref.at[:, x_from : x_from + x_n, 4 + z_from : 4 + z_from + z_n],
            dst_ref=raw_ref.at[:, x_to : x_to + x_n, row : row + z_n],
            send_sem=send.at[i],
            recv_sem=recv.at[i],
            device_id=(me_x + a, me_y + b, me_z + c),
            device_id_type=MESH,
        )

    def each(a, act, sign=1):
        for b, c in YZ if sign == 1 else YZ[::-1]:
            if (a, b, c) != (0, 0, 0):
                when(there(b, c, sign), lambda b=b, c=c: act(copy((a, b, c))))

    start, sent, got = (lambda x: x.start()), (lambda x: x.wait_send()), (lambda x: x.wait_recv())
    even = lax.rem(me_x, 2) == 0

    def near_all(act, sign=1):
        each(0, act, sign)
        pl.when(even == (sign == 1))(lambda: each(1, act, sign))
        pl.when(even == (sign != 1))(lambda: each(-1, act, sign))

    def far_all(act, sign=1):
        pl.when(me_x == (1 if sign == 1 else 2))(lambda: each(1, act, sign))
        pl.when(me_x == (2 if sign == 1 else 1))(lambda: each(-1, act, sign))

    def far_inner():
        pl.semaphore_wait(barrier, count(YZ))
        far_all(start)

    def far():
        pl.when(inner)(far_inner)

    def near_outer():
        pl.semaphore_wait(barrier, count(around) + count(YZ))
        pl.semaphore_signal(near_go, inc=1, device_id=(mate, me_y, me_z), device_id_type=MESH)

    def near():
        pl.when(~inner)(near_outer)
        pl.when(inner)(lambda: pl.semaphore_wait(near_go, 1))
        near_all(start)

    def near_got():
        near_all(got, -1)

    def far_got():
        far_all(got, -1)

    def all_sent():
        near_all(sent)
        far_all(sent)

    return enter, near, far, near_got, far_got, all_sent


def pair_density(centre, near):
    sep = [n - c for n, c in zip(near, centre)]
    dist_sq = sep[0] * sep[0] + sep[1] * sep[1] + sep[2] * sep[2]
    inside = jnp.maximum(1.0 - dist_sq, 0.0)
    inverse = lax.rsqrt(dist_sq)
    radius = dist_sq * inverse
    part = jnp.exp2(K_DENS * radius) * inside
    return sep, inside, inverse, radius, part


def pair_all(centre, near):
    sep, inside, inverse, radius, part = pair_density(centre, near)
    nearer = jnp.exp2(K_BOND * radius + C_BOND)
    less = nearer - 2.0
    near_in = nearer * inside
    over = inside * inverse
    pull_bond = near_in * ((nearer - 1.0) * over + (FOUR / (2.0 * MORSE)) * less)
    pull_dens = part * (over + FOUR / DECAY)
    return sep, part * inside, near_in * inside * less, pull_bond, pull_dens


def atoms(sizes, pos_ref, occ_ref, force_ref, energy_ref, raw, occ_v, rolled, moved, centres, slope, slope_rolled, slope_moved, density, bond, pull, edge_bonds, weighted, local, send, recv, near_go):
    n_x, n_y, n_z = sizes
    me_x, me_y, me_z = (lax.axis_index(a) for a in ("gx", "gy", "gz"))
    enter, near, far, near_got, far_got, all_sent = exchange(sizes, raw, send, recv, near_go)
    get_pos = pltpu.make_async_copy(pos_ref.at[:, :, 0], raw.at[:, 2:6, 5:7], local.at[0])
    get_occ = pltpu.make_async_copy(occ_ref.at[:, 0], occ_v, local.at[1])
    get_pos.start()
    get_occ.start()

    def load():
        get_occ.wait()
        get_pos.wait()
        for t in range(4):
            empty = jnp.where(occ_v[t] != 0, 0.0, far_away)
            raw[0, 2 + t, 5:7] = raw[0, 2 + t, 5:7] + empty

    ahead = me_x < 2
    most = me_y < n_y // 2
    least = me_y >= (5 * n_y) // 8
    at_once = (me_x == 2) & most

    def send_first():
        load()
        far()
        enter()

    def greet_first():
        enter()
        load()

    pl.when(at_once)(send_first)
    pl.when(~at_once)(greet_first)
    pl.when(~ahead & ~most)(far)
    near()

    nothing = lambda *s: jnp.zeros(s, jnp.float32)

    def blank_x(t):
        def run():
            raw[:, t : t + 2] = nothing(3, 2, 16, 128)

        return run

    def blank_rows(rows):
        def run():
            for r in rows:
                raw[:, :, r : r + 1] = nothing(3, 8, 1, 128)

        return run

    pl.when(me_x == 0)(blank_x(0))
    pl.when(me_x == n_x - 1)(blank_x(6))
    pl.when(me_y == 0)(blank_rows((0, 1, 2, 3)))
    pl.when(me_y == n_y - 1)(blank_rows((8, 9, 10, 11)))
    pl.when(me_z == 0)(blank_rows((0, 4, 8)))
    pl.when(me_z == n_z - 1)(blank_rows((3, 7, 11)))

    row, lane = iotas()
    turn = turn_indices()
    third = (lane % 32) // 8
    quarter = lane // 32
    out_z = ((me_z == 0) & (third == 0)) | ((me_z == n_z - 1) & (third == 3))
    far_z = jnp.where(out_z, far_away, 0.0)
    shift_z = (third - 1).astype(jnp.float32) * TILE_YZ
    odds = [(quarter + lane + a) % 2 == 1 for a in (0, 1)]
    unit = 1.0 / cut_radius

    reach = jnp.where(ahead, quarter, 3 - quarter)

    def place(k, n):
        return jnp.where(ahead, k, n - 1 - k)

    planes = [((third + row) % 4) * 32 + ((quarter + jnp.where(ahead, a, 4 - a)) % 4) * 8 + lane % 8 for a in range(4)]

    near_got()

    def take_tile(k):
        t = place(k, 8)
        out_x = ((me_x == 0) & (t < 2)) | ((me_x == n_x - 1) & (t > 5))
        far_x = jnp.where(out_x, far_away, 0.0) + (t - 2).astype(jnp.float32) * TILE_X
        for half in range(2):
            rows = slice(8 * half, 8 * half + 8)
            tile_y = 2 * half + row // 4
            out_y = ((me_y == 0) & (tile_y == 0)) | ((me_y == n_y - 1) & (tile_y == 2))
            shifts = [
                far_z + jnp.where(out_y, far_away, 0.0) + far_x,
                (tile_y - 1).astype(jnp.float32) * TILE_YZ,
                shift_z,
            ]
            for c in range(3):
                v = pick(pick(raw[c, t, rows], turn[0], 1), turn[1], 0)
                for a in range(4):
                    rolled[c, a, k, rows] = (pick(v, planes[a], 1) + shifts[c]) * unit

    def roll_planes(v, put):
        back, half, on = (pltpu.roll(v, 32 * m, 1) for m in (1, 2, 3))
        put(1)[...] = jnp.where(ahead, on, back)
        put(2)[...] = half
        put(3)[...] = jnp.where(ahead, back, on)

    def crossing(a):
        return reach + a > 3 if a > 0 else reach + a < 0

    def move_tile(k, shifts):
        for a in shifts:
            for c in range(3):
                for half in range(2):
                    rows = slice(8 * half, 8 * half + 8)
                    other = k + 2 if a > 0 else k
                    moved[c, a + 3, k, rows] = jnp.where(
                        crossing(a), rolled[c, a % 4, other, rows], rolled[c, a % 4, k + 1, rows]
                    )

    def roll_slope(k, value):
        slope[k, 2:10] = value
        roll_planes(value, lambda a: slope_rolled.at[a, k])

    def move_slope(k, shifts):
        for a in shifts:
            other = k + 1 if a > 0 else k - 1
            slope_moved[a + 3, k, 2:10] = jnp.where(
                crossing(a), slope_rolled[a % 4, other], slope_rolled[a % 4, k]
            )

    def rows_of(get, a, b):
        if b % 2 == 0:
            r = 2 + b // 2
            return [x[r : r + 8] for x in get]
        r = 2 + (b + 1) // 2
        return [jnp.where(odds[a % 2], x[r - 1 : r + 7], x[r : r + 8]) for x in get]

    def near_of(k, a, b):
        return rows_of([moved.at[c, a + 3, k] if a else rolled.at[c, 0, k + 1] for c in range(3)], a, b)

    def slope_of(k, a, b):
        return rows_of([slope_moved.at[a + 3, k] if a else slope.at[k]], a, b)[0]

    def centre_of(k, dz):
        return [pltpu.roll(rolled[c, 0, k + 1, 2:10], dz % 128, 1) if dz else rolled[c, 0, k + 1, 2:10] for c in range(3)]

    def home(x, dz):
        return pltpu.roll(x, (-dz) % 128, 1) if dz else x

    def slope_value(k, total):
        total = total * DENS_SCALE
        value = -0.5 * lax.rsqrt(total + 0.5) + 0.004 * total
        return jnp.where(rolled[0, 0, k + 1, 2:10] < 0.5 * far_away / cut_radius, value, 0.0)

    def ghost_density(k):
        total = nothing(8, 128)
        for dz in ZS:
            centre = centre_of(k, dz)
            here = nothing(8, 128)
            for a, b in BY_Z[dz]:
                _, inside, _, _, part = pair_density(centre, near_of(k, a, b))
                here = here + part * inside
            total = total + home(here, dz)
        return total

    def own_pairs(k):
        totals = [nothing(8, 128)] * 8
        for dz in ZS:
            centre = centre_of(k, dz)
            here = [nothing(8, 128)] * 8
            for a, b in BY_Z[dz]:
                sep, dens, bonding, pull_bond, pull_dens = pair_all(centre, near_of(k, a, b))
                here[0] = here[0] + dens
                here[1] = here[1] + bonding
                for c in range(3):
                    here[2 + c] = here[2 + c] + pull_bond * sep[c]
                    w = pull_dens * sep[c]
                    here[5 + c] = here[5 + c] + w
                    weighted[c, ORDER[a, b, dz], k] = w
            totals = [x + home(y, dz) for x, y in zip(totals, here)]
        return totals

    def edge_pairs(wanted, add):
        totals = [nothing(8, 128)] * 2
        for i, dz in enumerate(ZS):
            centre = [centres[c, i] for c in range(3)]
            here = [nothing(8, 128)] * 2
            bonds = [edge_bonds[c, i] if add else nothing(8, 128) for c in range(3)]
            for a, b in BY_Z[dz]:
                if not wanted(a):
                    continue
                sep, dens, bonding, pull_bond, pull_dens = pair_all(centre, near_of(4, a, b))
                here = [here[0] + dens, here[1] + bonding]
                for c in range(3):
                    bonds[c] = bonds[c] + pull_bond * sep[c]
                    weighted[c, ORDER[a, b, dz], 4] = pull_dens * sep[c]
            totals = [x + home(y, dz) for x, y in zip(totals, here)]
            for c in range(3):
                edge_bonds[c, i] = bonds[c]
        if add:
            totals = [totals[0] + density[4], totals[1] + bond[4]]
        density[4], bond[4] = totals
        return totals[0]

    def edge_pulls(value):
        totals = [nothing(8, 128)] * 3
        for i, dz in enumerate(ZS):
            own = pltpu.roll(value, dz % 128, 1) if dz else value
            here = [nothing(8, 128)] * 3
            for a, b in BY_Z[dz]:
                both = own + slope_of(4, a, b)
                for c in range(3):
                    here[c] = here[c] + both * weighted[c, ORDER[a, b, dz], 4]
            for c in range(3):
                totals[c] = totals[c] + home(PULL_BOND * edge_bonds[c, i] + PULL_DENS * here[c], dz)
        for c in range(3):
            pull[c, 4] = totals[c]

    def slope_pulls(k, wanted):
        totals = [nothing(8, 128)] * 3
        for dz in ZS:
            here = [nothing(8, 128)] * 3
            for a, b in BY_Z[dz]:
                if not wanted(a):
                    continue
                s = slope_of(k, a, b)
                for c in range(3):
                    here[c] = here[c] + s * weighted[c, ORDER[a, b, dz], k]
            totals = [x + home(y, dz) for x, y in zip(totals, here)]
        return totals

    def keep(k, totals, value):
        density[k] = totals[0]
        bond[k] = totals[1]
        for c in range(3):
            pull[c, k] = PULL_BOND * totals[2 + c] + PULL_DENS * (value * totals[5 + c])

    def add_pulls(k, totals):
        for c in range(3):
            pull[c, k] = pull[c, k] + PULL_DENS * totals[c]

    every, behind, beyond = (lambda a: True), (lambda a: a <= 0), (lambda a: a > 0)
    both_ways = (-3, -2, -1, 1, 2, 3)

    def loop(first, last, act):
        def run(k, carry):
            act(k)
            return carry

        lax.fori_loop(first, last, run, 0)

    slope[...] = nothing(6, 16, 128)
    slope_moved[...] = nothing(7, 6, 16, 128)
    loop(0, 6, take_tile)
    pl.when(ahead & least)(far)
    loop(0, 4, lambda k: move_tile(k, both_ways))
    move_tile(4, (-3, -2, -1))
    roll_slope(0, slope_value(0, ghost_density(0)))

    def own_whole(k):
        totals = own_pairs(k)
        value = slope_value(k, totals[0])
        keep(k, totals, value)
        roll_slope(k, value)

    loop(1, 4, own_whole)
    pl.when(ahead & ~least & ~most)(far)
    loop(1, 3, lambda k: move_slope(k, both_ways))
    move_slope(3, (-3, -2, -1))
    loop(1, 3, lambda k: add_pulls(k, slope_pulls(k, every)))
    add_pulls(3, slope_pulls(3, behind))
    for i, dz in enumerate(ZS):
        v = centre_of(4, dz)
        for c in range(3):
            centres[c, i] = v[c]

    edge_pairs(behind, False)

    pl.when(ahead & most)(far)
    all_sent()
    far_got()

    for k in (6, 7):
        take_tile(k)
    move_tile(4, (1, 2, 3))
    move_tile(5, both_ways)
    value = slope_value(4, edge_pairs(beyond, True))
    roll_slope(4, value)
    roll_slope(5, slope_value(5, ghost_density(5)))
    move_slope(4, both_ways)
    edge_pulls(value)
    move_slope(3, (1, 2, 3))
    add_pulls(3, slope_pulls(3, beyond))

    first_part, back, back_rows, back_slots = back_indices()

    def native(at):
        v = [at(place(p, 4) + 1) for p in range(4)]
        v = [pick(x, back, 1) for x in v]
        v = [jnp.where(first_part, v[2 * h], v[2 * h + 1]) for h in range(2)]
        v = [pick(x, back_rows, 0) for x in v]
        return pick(jnp.where(row < 4, v[0], v[1]), back_slots, 1)

    def store(dst, v):
        for t in range(4):
            dst[t, 0] = jnp.where(occ_v[t] != 0, v[2 * t : 2 * t + 2], 0.0)

    for c in range(3):
        store(force_ref.at[c], native(lambda k: pull[c, k]))

    def energy_of(k):
        d = density[k] * DENS_SCALE
        return BOND_SCALE * bond[k] - jnp.sqrt(d + 0.5) + 0.002 * d * d

    store(energy_ref, native(energy_of))


def put_out(force_in, energy_in, force_ref, energy_ref, sems):
    copies = [
        pltpu.make_async_copy(force_in, force_ref, sems.at[0]),
        pltpu.make_async_copy(energy_in, energy_ref, sems.at[1]),
    ]
    for x in copies:
        x.start()
    for x in copies:
        x.wait()


def scratch():
    f32 = lambda *s: pltpu.VMEM(s, jnp.float32)
    return [
        f32(3, 8, 16, 128),
        pltpu.VMEM((4, 2, 128), jnp.int32),
        f32(3, 4, 8, 16, 128),
        f32(3, 7, 6, 16, 128),
        f32(3, len(ZS), 8, 128),
        f32(6, 16, 128),
        f32(4, 6, 8, 128),
        f32(7, 6, 16, 128),
        f32(6, 8, 128),
        f32(6, 8, 128),
        f32(3, 6, 8, 128),
        f32(3, len(ZS), 8, 128),
        f32(3, len(VECTORS), 6, 8, 128),
        pltpu.SemaphoreType.DMA((2,)),
        pltpu.SemaphoreType.DMA((len(NEXT),)),
        pltpu.SemaphoreType.DMA((len(NEXT),)),
        pltpu.SemaphoreType.REGULAR,
    ]


def solution(mesh):
    sizes = tuple(mesh.shape[a] for a in ("gx", "gy", "gz"))

    def step(positions, occupied):
        positions, occupied = (pltpu.with_memory_space_constraint(x, pltpu.HBM) for x in (positions, occupied))
        found = pl.pallas_call(
            lambda *refs: atoms(sizes, *refs),
            out_shape=(pltpu.VMEM((3, 4, 1, 2, 128), jnp.float32), pltpu.VMEM((4, 1, 2, 128), jnp.float32)),
            in_specs=[pl.BlockSpec(memory_space=pl.ANY)] * 2,
            out_specs=[pl.BlockSpec(memory_space=pltpu.VMEM)] * 2,
            scratch_shapes=scratch(),
            compiler_params=pltpu.CompilerParams(
                collective_id=0, has_side_effects=True, vmem_limit_bytes=40 * 2**20
            ),
        )(positions, occupied)
        found = [pltpu.with_memory_space_constraint(x, pltpu.VMEM) for x in found]
        return pl.pallas_call(
            put_out,
            out_shape=[jax.ShapeDtypeStruct(x.shape, x.dtype) for x in found],
            in_specs=[pl.BlockSpec(memory_space=pltpu.VMEM)] * 2,
            out_specs=[pl.BlockSpec(memory_space=pl.ANY)] * 2,
            scratch_shapes=[pltpu.SemaphoreType.DMA((2,))],
        )(*found)

    in_specs = (P(None, "gx", "gy", "gz", None), P("gx", "gy", "gz", None))
    out_specs = (P(None, "gx", "gy", "gz", None), P("gx", "gy", "gz", None))
    return jax.shard_map(step, mesh=mesh, in_specs=in_specs, out_specs=out_specs, check_vma=False)
```

```python
import math

import jax
import jax.numpy as jnp
from jax import lax
from jax.experimental import pallas as pl
from jax.experimental.pallas import tpu as pltpu
from jax.sharding import PartitionSpec as P

MESH = pl.DeviceIdType.MESH

lattice_step = 3.615
cut_radius = 4.9
far_away = 1000.0

TILE_X = 2 * lattice_step
TILE_YZ = 4 * lattice_step
REACH = 3


def displacements():
    found = []
    near = lambda n: max(0.0, abs(n) * 0.5 * lattice_step - 0.7) ** 2
    for a in range(-4, 5):
        for b in range(-4, 5):
            for c in range(-4, 5):
                if (a + b + c) % 2 == 0 and (a, b, c) != (0, 0, 0):
                    if near(a) + near(b) + near(c) < cut_radius * cut_radius + 0.01:
                        found.append((a, b, c))
    return found


VECTORS = displacements()
ZS = sorted({v[2] for v in VECTORS})
BY_Z = {dz: [(v[0], v[1]) for v in VECTORS if v[2] == dz] for dz in ZS}
ORDER = {v: i for i, v in enumerate([(a, b, dz) for dz in ZS for a, b in BY_Z[dz]])}

LOG2E = 1.0 / math.log(2.0)
DECAY = 5.85 / 2.556
MORSE = 1.36
K_DENS = -DECAY * cut_radius * LOG2E
DENS_SCALE = math.exp(5.85)
K_BOND = -MORSE * cut_radius * LOG2E
C_BOND = MORSE * 2.556 * LOG2E
FOUR = 4.0 / cut_radius
BOND_SCALE = 0.5 * 0.3
PULL_BOND = -0.3 * 2.0 * MORSE
PULL_DENS = -DECAY * DENS_SCALE


def iotas():
    return (
        lax.broadcasted_iota(jnp.int32, (8, 128), 0),
        lax.broadcasted_iota(jnp.int32, (8, 128), 1),
    )


def pick(x, idx, axis):
    return jnp.take_along_axis(x, idx, axis=axis, mode="promise_in_bounds")


def turn_indices():
    row, lane = iotas()
    quarter, rest = lane // 32, lane % 32
    xs, zs = rest // 8, rest % 8
    y = (quarter - row % 4 + 4) % 4
    basis = jnp.where(xs % 2 == 0, 3 * (zs % 2), 1 + zs % 2)
    first = (xs // 2) * 64 + y * 16 + (zs // 2) * 4 + basis
    second = (row // 4) * 4 + (quarter - row % 4 + 4) % 4
    return first, second


def back_indices():
    row, lane = iotas()
    quarter, rest = lane // 32, lane % 32
    part = (quarter - row + 10) % 4
    first = (rest // 8) * 32 + (part % 2 + 1) * 8 + lane % 8
    second = 2 + (quarter - row % 4 + 4) % 4
    basis = lane % 4
    xs = 2 * (lane // 64) + jnp.where((basis == 1) | (basis == 2), 1, 0)
    zs = 2 * ((lane // 4) % 4) + basis // 2
    third = (((lane // 16) % 4 + row) % 4) * 32 + xs * 8 + zs
    return part < 2, first, second, third


YZ = sorted(((b, c) for b in (-1, 0, 1) for c in (-1, 0, 1)), key=lambda v: -abs(v[0]) - abs(v[1]))


def exchange(sizes, raw_ref, counted, send, recv, near_go):
    n_x, n_y, n_z = sizes
    me_x, me_y, me_z = (lax.axis_index(a) for a in ("gx", "gy", "gz"))
    inner = (me_x == 1) | (me_x == 2)
    low_pair = me_x < 2
    my_outer = jnp.where(low_pair, 0, 3)
    mate = jnp.where(low_pair, 1 - me_x, 5 - me_x)
    barrier = pltpu.get_barrier_semaphore()

    def there(b, c, sign=1):
        ok = []
        for step, me, n in ((b * sign, me_y, n_y), (c * sign, me_z, n_z)):
            if step == 1:
                ok.append(me < n - 1)
            if step == -1:
                ok.append(me > 0)
        return ok

    def when(conditions, act):
        if not conditions:
            return act()
        both = conditions[0]
        for x in conditions[1:]:
            both = both & x
        pl.when(both)(act)

    def count(steps):
        total = 0
        for b, c in steps:
            ok = there(b, c)
            if not ok:
                total = total + 1
                continue
            both = ok[0]
            for x in ok[1:]:
                both = both & x
            total = total + both.astype(jnp.int32)
        return total

    def greet(x, b, c):
        pl.semaphore_signal(
            barrier, inc=1, device_id=(x, me_y + b, me_z + c), device_id_type=MESH
        )

    around = [v for v in YZ if v != (0, 0)]

    def enter():
        def as_inner():
            for b, c in YZ:
                when(there(b, c), lambda b=b, c=c: greet(3 - me_x, b, c))
            greet(mate, 0, 0)

        pl.when(inner)(as_inner)
        for b, c in around:
            when(there(b, c), lambda b=b, c=c: greet(my_outer, b, c))

    def copy(v, part):
        a, b, c = v
        x_from, x_to, x_n = {0: (2, 2, 4), 1: (4, 0, 2), -1: (2, 6, 2)}[a]
        z_from, z_to, z_n = {0: (1, 1, 2), 1: (2, 0, 1), -1: (1, 3, 1)}[c]
        row = 4 * (1 - b) + z_to
        return pltpu.make_async_remote_copy(
            src_ref=raw_ref.at[:, x_from : x_from + x_n, 4 + z_from : 4 + z_from + z_n],
            dst_ref=raw_ref.at[:, x_to : x_to + x_n, row : row + z_n],
            send_sem=send.at[part],
            recv_sem=recv.at[part],
            device_id=(me_x + a, me_y + b, me_z + c),
            device_id_type=MESH,
        )

    def start(a, part):
        for b, c in YZ:
            if (a, b, c) != (0, 0, 0):
                when(there(b, c), lambda b=b, c=c: copy((a, b, c), part).start())

    even = lax.rem(me_x, 2) == 0
    end_y, end_z = (me_y == 0) | (me_y == n_y - 1), (me_z == 0) | (me_z == n_z - 1)

    def wait(sem, each, less=0):
        for last_y in (False, True):
            for last_z in (False, True):
                rows = each * (2 if last_y else 3) * (3 if last_z else 4) - less

                def run(rows=rows):
                    ref = counted.at[0:rows]
                    pltpu.make_async_copy(ref, ref, sem).wait()

                pl.when((end_y == last_y) & (end_z == last_z))(run)

    def far_inner():
        pl.semaphore_wait(barrier, count(YZ))
        pl.when(me_x == 1)(lambda: start(1, 1))
        pl.when(me_x == 2)(lambda: start(-1, 1))

    def far():
        pl.when(inner)(far_inner)

    def near_outer():
        pl.semaphore_wait(barrier, count(around) + count(YZ))
        pl.semaphore_signal(near_go, inc=1, device_id=(mate, me_y, me_z), device_id_type=MESH)

    def near():
        pl.when(~inner)(near_outer)
        pl.when(inner)(lambda: pl.semaphore_wait(near_go, 1))
        start(0, 0)
        pl.when(even)(lambda: start(1, 0))
        pl.when(~even)(lambda: start(-1, 0))

    def near_got():
        wait(recv.at[0], 18, 24)

    def far_got():
        pl.when(inner)(lambda: wait(recv.at[1], 6))

    def all_sent():
        wait(send.at[0], 18, 24)
        pl.when(inner)(lambda: wait(send.at[1], 6))

    return enter, near, far, near_got, far_got, all_sent


def pair_density(centre, near):
    sep = [n - c for n, c in zip(near, centre)]
    dist_sq = sep[0] * sep[0] + sep[1] * sep[1] + sep[2] * sep[2]
    inside = jnp.maximum(1.0 - dist_sq, 0.0)
    inverse = lax.rsqrt(dist_sq)
    radius = dist_sq * inverse
    part = jnp.exp2(K_DENS * radius) * inside
    return sep, inside, inverse, radius, part


def pair_all(centre, near):
    sep, inside, inverse, radius, part = pair_density(centre, near)
    nearer = jnp.exp2(K_BOND * radius + C_BOND)
    less = nearer - 2.0
    near_in = nearer * inside
    over = inside * inverse
    pull_bond = near_in * ((nearer - 1.0) * over + (FOUR / (2.0 * MORSE)) * less)
    pull_dens = part * (over + FOUR / DECAY)
    return sep, part * inside, near_in * inside * less, pull_bond, pull_dens


def atoms(sizes, pos_ref, occ_ref, force_ref, energy_ref, raw, occ_v, rolled, moved, centres, slope, slope_rolled, slope_moved, density, bond, pull, edge_bonds, weighted, counted, local, send, recv, near_go):
    n_x, n_y, n_z = sizes
    me_x, me_y, me_z = (lax.axis_index(a) for a in ("gx", "gy", "gz"))
    enter, near, far, near_got, far_got, all_sent = exchange(sizes, raw, counted, send, recv, near_go)
    get_pos = pltpu.make_async_copy(pos_ref.at[:, :, 0], raw.at[:, 2:6, 5:7], local.at[0])
    get_occ = pltpu.make_async_copy(occ_ref.at[:, 0], occ_v, local.at[1])
    get_pos.start()
    get_occ.start()

    def load():
        get_occ.wait()
        get_pos.wait()
        for t in range(4):
            empty = jnp.where(occ_v[t] != 0, 0.0, far_away)
            raw[0, 2 + t, 5:7] = raw[0, 2 + t, 5:7] + empty

    ahead = me_x < 2
    most = me_y < n_y // 2
    least = me_y >= (5 * n_y) // 8
    at_once = (me_x == 2) & most

    def send_first():
        load()
        far()
        enter()

    def greet_first():
        enter()
        load()

    pl.when(at_once)(send_first)
    pl.when(~at_once)(greet_first)
    pl.when(~ahead & ~most)(far)
    near()

    nothing = lambda *s: jnp.zeros(s, jnp.float32)

    def blank_x(t):
        def run():
            raw[:, t : t + 2] = nothing(3, 2, 16, 128)

        return run

    def blank_rows(rows):
        def run():
            for r in rows:
                raw[:, :, r : r + 1] = nothing(3, 8, 1, 128)

        return run

    pl.when(me_x == 0)(blank_x(0))
    pl.when(me_x == n_x - 1)(blank_x(6))
    pl.when(me_y == 0)(blank_rows((0, 1, 2, 3)))
    pl.when(me_y == n_y - 1)(blank_rows((8, 9, 10, 11)))
    pl.when(me_z == 0)(blank_rows((0, 4, 8)))
    pl.when(me_z == n_z - 1)(blank_rows((3, 7, 11)))

    row, lane = iotas()
    turn = turn_indices()
    third = (lane % 32) // 8
    quarter = lane // 32
    out_z = ((me_z == 0) & (third == 0)) | ((me_z == n_z - 1) & (third == 3))
    far_z = jnp.where(out_z, far_away, 0.0)
    shift_z = (third - 1).astype(jnp.float32) * TILE_YZ
    odds = [(quarter + lane + a) % 2 == 1 for a in (0, 1)]
    unit = 1.0 / cut_radius

    reach = jnp.where(ahead, quarter, 3 - quarter)

    def place(k, n):
        return jnp.where(ahead, k, n - 1 - k)

    planes = [((third + row) % 4) * 32 + ((quarter + jnp.where(ahead, a, 4 - a)) % 4) * 8 + lane % 8 for a in range(4)]

    near_got()

    def take_tile(k):
        t = place(k, 8)
        out_x = ((me_x == 0) & (t < 2)) | ((me_x == n_x - 1) & (t > 5))
        far_x = jnp.where(out_x, far_away, 0.0) + (t - 2).astype(jnp.float32) * TILE_X
        for half in range(2):
            rows = slice(8 * half, 8 * half + 8)
            tile_y = 2 * half + row // 4
            out_y = ((me_y == 0) & (tile_y == 0)) | ((me_y == n_y - 1) & (tile_y == 2))
            shifts = [
                far_z + jnp.where(out_y, far_away, 0.0) + far_x,
                (tile_y - 1).astype(jnp.float32) * TILE_YZ,
                shift_z,
            ]
            for c in range(3):
                v = pick(pick(raw[c, t, rows], turn[0], 1), turn[1], 0)
                for a in range(4):
                    rolled[c, a, k, rows] = (pick(v, planes[a], 1) + shifts[c]) * unit

    def roll_planes(v, put):
        back, half, on = (pltpu.roll(v, 32 * m, 1) for m in (1, 2, 3))
        put(1)[...] = jnp.where(ahead, on, back)
        put(2)[...] = half
        put(3)[...] = jnp.where(ahead, back, on)

    def crossing(a):
        return reach + a > 3 if a > 0 else reach + a < 0

    def move_tile(k, shifts):
        for a in shifts:
            for c in range(3):
                for half in range(2):
                    rows = slice(8 * half, 8 * half + 8)
                    other = k + 2 if a > 0 else k
                    moved[c, a + 3, k, rows] = jnp.where(
                        crossing(a), rolled[c, a % 4, other, rows], rolled[c, a % 4, k + 1, rows]
                    )

    def roll_slope(k, value):
        slope[k, 2:10] = value
        roll_planes(value, lambda a: slope_rolled.at[a, k])

    def move_slope(k, shifts):
        for a in shifts:
            other = k + 1 if a > 0 else k - 1
            slope_moved[a + 3, k, 2:10] = jnp.where(
                crossing(a), slope_rolled[a % 4, other], slope_rolled[a % 4, k]
            )

    def rows_of(get, a, b):
        if b % 2 == 0:
            r = 2 + b // 2
            return [x[r : r + 8] for x in get]
        r = 2 + (b + 1) // 2
        return [jnp.where(odds[a % 2], x[r - 1 : r + 7], x[r : r + 8]) for x in get]

    def near_of(k, a, b):
        return rows_of([moved.at[c, a + 3, k] if a else rolled.at[c, 0, k + 1] for c in range(3)], a, b)

    def slope_of(k, a, b):
        return rows_of([slope_moved.at[a + 3, k] if a else slope.at[k]], a, b)[0]

    def centre_of(k, dz):
        return [pltpu.roll(rolled[c, 0, k + 1, 2:10], dz % 128, 1) if dz else rolled[c, 0, k + 1, 2:10] for c in range(3)]

    def home(x, dz):
        return pltpu.roll(x, (-dz) % 128, 1) if dz else x

    def slope_value(k, total):
        total = total * DENS_SCALE
        value = -0.5 * lax.rsqrt(total + 0.5) + 0.004 * total
        return jnp.where(rolled[0, 0, k + 1, 2:10] < 0.5 * far_away / cut_radius, value, 0.0)

    def ghost_density(k):
        total = nothing(8, 128)
        for dz in ZS:
            centre = centre_of(k, dz)
            here = nothing(8, 128)
            for a, b in BY_Z[dz]:
                _, inside, _, _, part = pair_density(centre, near_of(k, a, b))
                here = here + part * inside
            total = total + home(here, dz)
        return total

    def own_pairs(k):
        totals = [nothing(8, 128)] * 8
        for dz in ZS:
            centre = centre_of(k, dz)
            here = [nothing(8, 128)] * 8
            for a, b in BY_Z[dz]:
                sep, dens, bonding, pull_bond, pull_dens = pair_all(centre, near_of(k, a, b))
                here[0] = here[0] + dens
                here[1] = here[1] + bonding
                for c in range(3):
                    here[2 + c] = here[2 + c] + pull_bond * sep[c]
                    w = pull_dens * sep[c]
                    here[5 + c] = here[5 + c] + w
                    weighted[c, ORDER[a, b, dz], k] = w
            totals = [x + home(y, dz) for x, y in zip(totals, here)]
        return totals

    def edge_pairs(wanted, add):
        totals = [nothing(8, 128)] * 2
        for i, dz in enumerate(ZS):
            centre = [centres[c, i] for c in range(3)]
            here = [nothing(8, 128)] * 2
            bonds = [edge_bonds[c, i] if add else nothing(8, 128) for c in range(3)]
            for a, b in BY_Z[dz]:
                if not wanted(a):
                    continue
                sep, dens, bonding, pull_bond, pull_dens = pair_all(centre, near_of(4, a, b))
                here = [here[0] + dens, here[1] + bonding]
                for c in range(3):
                    bonds[c] = bonds[c] + pull_bond * sep[c]
                    weighted[c, ORDER[a, b, dz], 4] = pull_dens * sep[c]
            totals = [x + home(y, dz) for x, y in zip(totals, here)]
            for c in range(3):
                edge_bonds[c, i] = bonds[c]
        if add:
            totals = [totals[0] + density[4], totals[1] + bond[4]]
        density[4], bond[4] = totals
        return totals[0]

    def edge_pulls(value):
        totals = [nothing(8, 128)] * 3
        for i, dz in enumerate(ZS):
            own = pltpu.roll(value, dz % 128, 1) if dz else value
            here = [nothing(8, 128)] * 3
            for a, b in BY_Z[dz]:
                both = own + slope_of(4, a, b)
                for c in range(3):
                    here[c] = here[c] + both * weighted[c, ORDER[a, b, dz], 4]
            for c in range(3):
                totals[c] = totals[c] + home(PULL_BOND * edge_bonds[c, i] + PULL_DENS * here[c], dz)
        for c in range(3):
            pull[c, 4] = totals[c]

    def slope_pulls(k, wanted):
        totals = [nothing(8, 128)] * 3
        for dz in ZS:
            here = [nothing(8, 128)] * 3
            for a, b in BY_Z[dz]:
                if not wanted(a):
                    continue
                s = slope_of(k, a, b)
                for c in range(3):
                    here[c] = here[c] + s * weighted[c, ORDER[a, b, dz], k]
            totals = [x + home(y, dz) for x, y in zip(totals, here)]
        return totals

    def keep(k, totals, value):
        density[k] = totals[0]
        bond[k] = totals[1]
        for c in range(3):
            pull[c, k] = PULL_BOND * totals[2 + c] + PULL_DENS * (value * totals[5 + c])

    def add_pulls(k, totals):
        for c in range(3):
            pull[c, k] = pull[c, k] + PULL_DENS * totals[c]

    every, behind, beyond = (lambda a: True), (lambda a: a <= 0), (lambda a: a > 0)
    both_ways = (-3, -2, -1, 1, 2, 3)

    def loop(first, last, act):
        def run(k, carry):
            act(k)
            return carry

        lax.fori_loop(first, last, run, 0)

    slope[...] = nothing(6, 16, 128)
    slope_moved[...] = nothing(7, 6, 16, 128)
    loop(0, 6, take_tile)
    pl.when(ahead & least)(far)
    loop(0, 4, lambda k: move_tile(k, both_ways))
    move_tile(4, (-3, -2, -1))
    roll_slope(0, slope_value(0, ghost_density(0)))

    def own_whole(k):
        totals = own_pairs(k)
        value = slope_value(k, totals[0])
        keep(k, totals, value)
        roll_slope(k, value)

    loop(1, 4, own_whole)
    pl.when(ahead & ~least & ~most)(far)
    loop(1, 3, lambda k: move_slope(k, both_ways))
    move_slope(3, (-3, -2, -1))
    loop(1, 3, lambda k: add_pulls(k, slope_pulls(k, every)))
    add_pulls(3, slope_pulls(3, behind))
    for i, dz in enumerate(ZS):
        v = centre_of(4, dz)
        for c in range(3):
            centres[c, i] = v[c]

    edge_pairs(behind, False)

    pl.when(ahead & most)(far)
    all_sent()
    far_got()

    for k in (6, 7):
        take_tile(k)
    move_tile(4, (1, 2, 3))
    move_tile(5, both_ways)
    value = slope_value(4, edge_pairs(beyond, True))
    roll_slope(4, value)
    roll_slope(5, slope_value(5, ghost_density(5)))
    move_slope(4, both_ways)
    edge_pulls(value)
    move_slope(3, (1, 2, 3))
    add_pulls(3, slope_pulls(3, beyond))

    first_part, back, back_rows, back_slots = back_indices()

    def native(at):
        v = [at(place(p, 4) + 1) for p in range(4)]
        v = [pick(x, back, 1) for x in v]
        v = [jnp.where(first_part, v[2 * h], v[2 * h + 1]) for h in range(2)]
        v = [pick(x, back_rows, 0) for x in v]
        return pick(jnp.where(row < 4, v[0], v[1]), back_slots, 1)

    def store(dst, v):
        for t in range(4):
            dst[t, 0] = jnp.where(occ_v[t] != 0, v[2 * t : 2 * t + 2], 0.0)

    for c in range(3):
        store(force_ref.at[c], native(lambda k: pull[c, k]))

    def energy_of(k):
        d = density[k] * DENS_SCALE
        return BOND_SCALE * bond[k] - jnp.sqrt(d + 0.5) + 0.002 * d * d

    store(energy_ref, native(energy_of))


def put_out(force_in, energy_in, force_ref, energy_ref, sems):
    copies = [
        pltpu.make_async_copy(force_in, force_ref, sems.at[0]),
        pltpu.make_async_copy(energy_in, energy_ref, sems.at[1]),
    ]
    for x in copies:
        x.start()
    for x in copies:
        x.wait()


def scratch():
    f32 = lambda *s: pltpu.VMEM(s, jnp.float32)
    return [
        f32(3, 8, 16, 128),
        pltpu.VMEM((4, 2, 128), jnp.int32),
        f32(3, 4, 8, 16, 128),
        f32(3, 7, 6, 16, 128),
        f32(3, len(ZS), 8, 128),
        f32(6, 16, 128),
        f32(4, 6, 8, 128),
        f32(7, 6, 16, 128),
        f32(6, 8, 128),
        f32(6, 8, 128),
        f32(3, 6, 8, 128),
        f32(3, len(ZS), 8, 128),
        f32(3, len(VECTORS), 6, 8, 128),
        f32(192, 128),
        pltpu.SemaphoreType.DMA((2,)),
        pltpu.SemaphoreType.DMA((2,)),
        pltpu.SemaphoreType.DMA((2,)),
        pltpu.SemaphoreType.REGULAR,
    ]


def solution(mesh):
    sizes = tuple(mesh.shape[a] for a in ("gx", "gy", "gz"))

    def step(positions, occupied):
        positions, occupied = (pltpu.with_memory_space_constraint(x, pltpu.HBM) for x in (positions, occupied))
        found = pl.pallas_call(
            lambda *refs: atoms(sizes, *refs),
            out_shape=(pltpu.VMEM((3, 4, 1, 2, 128), jnp.float32), pltpu.VMEM((4, 1, 2, 128), jnp.float32)),
            in_specs=[pl.BlockSpec(memory_space=pl.ANY)] * 2,
            out_specs=[pl.BlockSpec(memory_space=pltpu.VMEM)] * 2,
            scratch_shapes=scratch(),
            compiler_params=pltpu.CompilerParams(
                collective_id=0, has_side_effects=True, vmem_limit_bytes=40 * 2**20
            ),
        )(positions, occupied)
        found = [pltpu.with_memory_space_constraint(x, pltpu.VMEM) for x in found]
        return pl.pallas_call(
            put_out,
            out_shape=[jax.ShapeDtypeStruct(x.shape, x.dtype) for x in found],
            in_specs=[pl.BlockSpec(memory_space=pltpu.VMEM)] * 2,
            out_specs=[pl.BlockSpec(memory_space=pl.ANY)] * 2,
            scratch_shapes=[pltpu.SemaphoreType.DMA((2,))],
        )(*found)

    in_specs = (P(None, "gx", "gy", "gz", None), P("gx", "gy", "gz", None))
    out_specs = (P(None, "gx", "gy", "gz", None), P("gx", "gy", "gz", None))
    return jax.shard_map(step, mesh=mesh, in_specs=in_specs, out_specs=out_specs, check_vma=False)
```

```python
import math

import jax
import jax.numpy as jnp
from jax import lax
from jax.experimental import pallas as pl
from jax.experimental.pallas import tpu as pltpu
from jax.sharding import PartitionSpec as P

MESH = pl.DeviceIdType.MESH

lattice_step = 3.615
cut_radius = 4.9
far_away = 1000.0

TILE_X = 2 * lattice_step
TILE_YZ = 4 * lattice_step
REACH = 3


def displacements():
    found = []
    near = lambda n: max(0.0, abs(n) * 0.5 * lattice_step - 0.7) ** 2
    for a in range(-4, 5):
        for b in range(-4, 5):
            for c in range(-4, 5):
                if (a + b + c) % 2 == 0 and (a, b, c) != (0, 0, 0):
                    if near(a) + near(b) + near(c) < cut_radius * cut_radius + 0.01:
                        found.append((a, b, c))
    return found


VECTORS = displacements()
ZS = sorted({v[2] for v in VECTORS})
BY_Z = {dz: [(v[0], v[1]) for v in VECTORS if v[2] == dz] for dz in ZS}
ORDER = {v: i for i, v in enumerate([(a, b, dz) for dz in ZS for a, b in BY_Z[dz]])}

LOG2E = 1.0 / math.log(2.0)
DECAY = 5.85 / 2.556
MORSE = 1.36
K_DENS = -DECAY * cut_radius * LOG2E
DENS_SCALE = math.exp(5.85)
K_BOND = -MORSE * cut_radius * LOG2E
C_BOND = MORSE * 2.556 * LOG2E
FOUR = 4.0 / cut_radius
BOND_SCALE = 0.5 * 0.3
PULL_BOND = -0.3 * 2.0 * MORSE
PULL_DENS = -DECAY * DENS_SCALE


def iotas():
    return (
        lax.broadcasted_iota(jnp.int32, (8, 128), 0),
        lax.broadcasted_iota(jnp.int32, (8, 128), 1),
    )


def pick(x, idx, axis):
    return jnp.take_along_axis(x, idx, axis=axis, mode="promise_in_bounds")


def turn_indices():
    row, lane = iotas()
    quarter, rest = lane // 32, lane % 32
    xs, zs = rest // 8, rest % 8
    y = (quarter - row % 4 + 4) % 4
    basis = jnp.where(xs % 2 == 0, 3 * (zs % 2), 1 + zs % 2)
    first = (xs // 2) * 64 + y * 16 + (zs // 2) * 4 + basis
    second = (row // 4) * 4 + (quarter - row % 4 + 4) % 4
    return first, second


def back_indices():
    row, lane = iotas()
    quarter, rest = lane // 32, lane % 32
    part = (quarter - row + 10) % 4
    first = (rest // 8) * 32 + (part % 2 + 1) * 8 + lane % 8
    second = 2 + (quarter - row % 4 + 4) % 4
    basis = lane % 4
    xs = 2 * (lane // 64) + jnp.where((basis == 1) | (basis == 2), 1, 0)
    zs = 2 * ((lane // 4) % 4) + basis // 2
    third = (((lane // 16) % 4 + row) % 4) * 32 + xs * 8 + zs
    return part < 2, first, second, third


YZ = sorted(((b, c) for b in (-1, 0, 1) for c in (-1, 0, 1)), key=lambda v: -abs(v[0]) - abs(v[1]))


def exchange(sizes, pos_ref, occ_ref, raw_ref, far_occ, counted, send, recv, near_go):
    n_x, n_y, n_z = sizes
    me_x, me_y, me_z = (lax.axis_index(a) for a in ("gx", "gy", "gz"))
    inner = (me_x == 1) | (me_x == 2)
    low_pair = me_x < 2
    my_outer = jnp.where(low_pair, 0, 3)
    mate = jnp.where(low_pair, 1 - me_x, 5 - me_x)
    barrier = pltpu.get_barrier_semaphore()

    def there(b, c, sign=1):
        ok = []
        for step, me, n in ((b * sign, me_y, n_y), (c * sign, me_z, n_z)):
            if step == 1:
                ok.append(me < n - 1)
            if step == -1:
                ok.append(me > 0)
        return ok

    def when(conditions, act):
        if not conditions:
            return act()
        both = conditions[0]
        for x in conditions[1:]:
            both = both & x
        pl.when(both)(act)

    def count(steps):
        total = 0
        for b, c in steps:
            ok = there(b, c)
            if not ok:
                total = total + 1
                continue
            both = ok[0]
            for x in ok[1:]:
                both = both & x
            total = total + both.astype(jnp.int32)
        return total

    def greet(x, b, c):
        pl.semaphore_signal(
            barrier, inc=1, device_id=(x, me_y + b, me_z + c), device_id_type=MESH
        )

    around = [v for v in YZ if v != (0, 0)]

    def enter():
        def as_inner():
            for b, c in YZ:
                when(there(b, c), lambda b=b, c=c: greet(3 - me_x, b, c))
            greet(mate, 0, 0)

        pl.when(inner)(as_inner)
        for b, c in around:
            when(there(b, c), lambda b=b, c=c: greet(my_outer, b, c))

    def copies(v, part):
        a, b, c = v
        x_from, x_to, x_n = {0: (0, 2, 4), 1: (2, 0, 2), -1: (0, 6, 2)}[a]
        z_from, z_to, z_n = {0: (0, 1, 2), 1: (1, 0, 1), -1: (0, 3, 1)}[c]
        row = 4 * (1 - b) + z_to

        def remote(src, dst):
            return pltpu.make_async_remote_copy(
                src_ref=src,
                dst_ref=dst,
                send_sem=send.at[part],
                recv_sem=recv.at[part],
                device_id=(me_x + a, me_y + b, me_z + c),
                device_id_type=MESH,
            )

        dst = raw_ref.at[:, x_to : x_to + x_n, row : row + z_n]
        if part == 0:
            return [remote(raw_ref.at[:, 2 + x_from : 2 + x_from + x_n, 5 + z_from : 5 + z_from + z_n], dst)]
        at = (slice(x_from, x_from + x_n), 0, slice(z_from, z_from + z_n))
        return [
            remote(pos_ref.at[(slice(None), *at)], dst),
            remote(occ_ref.at[at], far_occ.at[:, row : row + z_n]),
        ]

    def start(a, part):
        for b, c in YZ:
            if (a, b, c) != (0, 0, 0):

                def run(v=(a, b, c)):
                    for x in copies(v, part):
                        x.start()

                when(there(b, c), run)

    even = lax.rem(me_x, 2) == 0
    end_y, end_z = (me_y == 0) | (me_y == n_y - 1), (me_z == 0) | (me_z == n_z - 1)

    def wait(sem, each, less=0):
        for last_y in (False, True):
            for last_z in (False, True):
                rows = each * (2 if last_y else 3) * (3 if last_z else 4) - less

                def run(rows=rows):
                    ref = counted.at[0:rows]
                    pltpu.make_async_copy(ref, ref, sem).wait()

                pl.when((end_y == last_y) & (end_z == last_z))(run)

    def far_inner():
        pl.semaphore_wait(barrier, count(YZ))
        pl.when(me_x == 1)(lambda: start(1, 1))
        pl.when(me_x == 2)(lambda: start(-1, 1))

    def far():
        pl.when(inner)(far_inner)

    def near_outer():
        pl.semaphore_wait(barrier, count(around) + count(YZ))
        pl.semaphore_signal(near_go, inc=1, device_id=(mate, me_y, me_z), device_id_type=MESH)

    def near():
        pl.when(~inner)(near_outer)
        pl.when(inner)(lambda: pl.semaphore_wait(near_go, 1))
        start(0, 0)
        pl.when(even)(lambda: start(1, 0))
        pl.when(~even)(lambda: start(-1, 0))

    def near_got():
        wait(recv.at[0], 18, 24)

    def far_got():
        pl.when(inner)(lambda: wait(recv.at[1], 8))

    def all_sent():
        wait(send.at[0], 18, 24)
        pl.when(inner)(lambda: wait(send.at[1], 8))

    return enter, near, far, near_got, far_got, all_sent


def pair_density(centre, near):
    sep = [n - c for n, c in zip(near, centre)]
    dist_sq = sep[0] * sep[0] + sep[1] * sep[1] + sep[2] * sep[2]
    inside = jnp.maximum(1.0 - dist_sq, 0.0)
    inverse = lax.rsqrt(dist_sq)
    radius = dist_sq * inverse
    part = jnp.exp2(K_DENS * radius) * inside
    return sep, inside, inverse, radius, part


def pair_all(centre, near):
    sep, inside, inverse, radius, part = pair_density(centre, near)
    nearer = jnp.exp2(K_BOND * radius + C_BOND)
    less = nearer - 2.0
    near_in = nearer * inside
    over = inside * inverse
    pull_bond = near_in * ((nearer - 1.0) * over + (FOUR / (2.0 * MORSE)) * less)
    pull_dens = part * (over + FOUR / DECAY)
    return sep, part * inside, near_in * inside * less, pull_bond, pull_dens


def atoms(sizes, pos_ref, occ_ref, force_ref, energy_ref, raw, occ_v, far_occ, rolled, moved, centres, slope, slope_rolled, slope_moved, density, bond, pull, edge_bonds, weighted, counted, local, send, recv, near_go):
    n_x, n_y, n_z = sizes
    me_x, me_y, me_z = (lax.axis_index(a) for a in ("gx", "gy", "gz"))
    enter, near, far, near_got, far_got, all_sent = exchange(sizes, pos_ref, occ_ref, raw, far_occ, counted, send, recv, near_go)
    get_pos = pltpu.make_async_copy(pos_ref.at[:, :, 0], raw.at[:, 2:6, 5:7], local.at[0])
    get_occ = pltpu.make_async_copy(occ_ref.at[:, 0], occ_v, local.at[1])
    far_occ[...] = jnp.ones((2, 16, 128), jnp.int32)
    get_pos.start()
    get_occ.start()

    def load():
        get_occ.wait()
        get_pos.wait()
        for t in range(4):
            empty = jnp.where(occ_v[t] != 0, 0.0, far_away)
            raw[0, 2 + t, 5:7] = raw[0, 2 + t, 5:7] + empty

    ahead = me_x < 2
    most = me_y < n_y // 2
    least = me_y >= (5 * n_y) // 8
    at_once = (me_x == 2) & most

    def send_first():
        far()
        load()
        enter()

    def greet_first():
        enter()
        load()

    pl.when(at_once)(send_first)
    pl.when(~at_once)(greet_first)
    pl.when(~ahead & ~most)(far)
    near()

    nothing = lambda *s: jnp.zeros(s, jnp.float32)

    def blank_x(t):
        def run():
            raw[:, t : t + 2] = nothing(3, 2, 16, 128)

        return run

    def blank_rows(rows):
        def run():
            for r in rows:
                raw[:, :, r : r + 1] = nothing(3, 8, 1, 128)

        return run

    pl.when(me_x == 0)(blank_x(0))
    pl.when(me_x == n_x - 1)(blank_x(6))
    pl.when(me_y == 0)(blank_rows((0, 1, 2, 3)))
    pl.when(me_y == n_y - 1)(blank_rows((8, 9, 10, 11)))
    pl.when(me_z == 0)(blank_rows((0, 4, 8)))
    pl.when(me_z == n_z - 1)(blank_rows((3, 7, 11)))

    row, lane = iotas()
    turn = turn_indices()
    third = (lane % 32) // 8
    quarter = lane // 32
    out_z = ((me_z == 0) & (third == 0)) | ((me_z == n_z - 1) & (third == 3))
    far_z = jnp.where(out_z, far_away, 0.0)
    shift_z = (third - 1).astype(jnp.float32) * TILE_YZ
    odds = [(quarter + lane + a) % 2 == 1 for a in (0, 1)]
    unit = 1.0 / cut_radius

    reach = jnp.where(ahead, quarter, 3 - quarter)

    def place(k, n):
        return jnp.where(ahead, k, n - 1 - k)

    planes = [((third + row) % 4) * 32 + ((quarter + jnp.where(ahead, a, 4 - a)) % 4) * 8 + lane % 8 for a in range(4)]

    near_got()

    def take_tile(k, occupied=None):
        t = place(k, 8)
        out_x = ((me_x == 0) & (t < 2)) | ((me_x == n_x - 1) & (t > 5))
        far_x = jnp.where(out_x, far_away, 0.0) + (t - 2).astype(jnp.float32) * TILE_X
        for half in range(2):
            rows = slice(8 * half, 8 * half + 8)
            tile_y = 2 * half + row // 4
            out_y = ((me_y == 0) & (tile_y == 0)) | ((me_y == n_y - 1) & (tile_y == 2))
            shifts = [
                far_z + jnp.where(out_y, far_away, 0.0) + far_x,
                (tile_y - 1).astype(jnp.float32) * TILE_YZ,
                shift_z,
            ]
            for c in range(3):
                v = raw[c, t, rows]
                if c == 0 and occupied is not None:
                    v = v + jnp.where(occupied[rows] != 0, 0.0, far_away)
                v = pick(pick(v, turn[0], 1), turn[1], 0)
                for a in range(4):
                    rolled[c, a, k, rows] = (pick(v, planes[a], 1) + shifts[c]) * unit

    def roll_planes(v, put):
        back, half, on = (pltpu.roll(v, 32 * m, 1) for m in (1, 2, 3))
        put(1)[...] = jnp.where(ahead, on, back)
        put(2)[...] = half
        put(3)[...] = jnp.where(ahead, back, on)

    def crossing(a):
        return reach + a > 3 if a > 0 else reach + a < 0

    def move_tile(k, shifts):
        for a in shifts:
            for c in range(3):
                for half in range(2):
                    rows = slice(8 * half, 8 * half + 8)
                    other = k + 2 if a > 0 else k
                    moved[c, a + 3, k, rows] = jnp.where(
                        crossing(a), rolled[c, a % 4, other, rows], rolled[c, a % 4, k + 1, rows]
                    )

    def roll_slope(k, value):
        slope[k, 2:10] = value
        roll_planes(value, lambda a: slope_rolled.at[a, k])

    def move_slope(k, shifts):
        for a in shifts:
            other = k + 1 if a > 0 else k - 1
            slope_moved[a + 3, k, 2:10] = jnp.where(
                crossing(a), slope_rolled[a % 4, other], slope_rolled[a % 4, k]
            )

    def rows_of(get, a, b):
        if b % 2 == 0:
            r = 2 + b // 2
            return [x[r : r + 8] for x in get]
        r = 2 + (b + 1) // 2
        return [jnp.where(odds[a % 2], x[r - 1 : r + 7], x[r : r + 8]) for x in get]

    def near_of(k, a, b):
        return rows_of([moved.at[c, a + 3, k] if a else rolled.at[c, 0, k + 1] for c in range(3)], a, b)

    def slope_of(k, a, b):
        return rows_of([slope_moved.at[a + 3, k] if a else slope.at[k]], a, b)[0]

    def centre_of(k, dz):
        return [pltpu.roll(rolled[c, 0, k + 1, 2:10], dz % 128, 1) if dz else rolled[c, 0, k + 1, 2:10] for c in range(3)]

    def home(x, dz):
        return pltpu.roll(x, (-dz) % 128, 1) if dz else x

    def slope_value(k, total):
        total = total * DENS_SCALE
        value = -0.5 * lax.rsqrt(total + 0.5) + 0.004 * total
        return jnp.where(rolled[0, 0, k + 1, 2:10] < 0.5 * far_away / cut_radius, value, 0.0)

    def ghost_density(k):
        total = nothing(8, 128)
        for dz in ZS:
            centre = centre_of(k, dz)
            here = nothing(8, 128)
            for a, b in BY_Z[dz]:
                _, inside, _, _, part = pair_density(centre, near_of(k, a, b))
                here = here + part * inside
            total = total + home(here, dz)
        return total

    def own_pairs(k):
        totals = [nothing(8, 128)] * 8
        for dz in ZS:
            centre = centre_of(k, dz)
            here = [nothing(8, 128)] * 8
            for a, b in BY_Z[dz]:
                sep, dens, bonding, pull_bond, pull_dens = pair_all(centre, near_of(k, a, b))
                here[0] = here[0] + dens
                here[1] = here[1] + bonding
                for c in range(3):
                    here[2 + c] = here[2 + c] + pull_bond * sep[c]
                    w = pull_dens * sep[c]
                    here[5 + c] = here[5 + c] + w
                    weighted[c, ORDER[a, b, dz], k] = w
            totals = [x + home(y, dz) for x, y in zip(totals, here)]
        return totals

    def edge_pairs(wanted, add):
        totals = [nothing(8, 128)] * 2
        for i, dz in enumerate(ZS):
            centre = [centres[c, i] for c in range(3)]
            here = [nothing(8, 128)] * 2
            bonds = [edge_bonds[c, i] if add else nothing(8, 128) for c in range(3)]
            for a, b in BY_Z[dz]:
                if not wanted(a):
                    continue
                sep, dens, bonding, pull_bond, pull_dens = pair_all(centre, near_of(4, a, b))
                here = [here[0] + dens, here[1] + bonding]
                for c in range(3):
                    bonds[c] = bonds[c] + pull_bond * sep[c]
                    weighted[c, ORDER[a, b, dz], 4] = pull_dens * sep[c]
            totals = [x + home(y, dz) for x, y in zip(totals, here)]
            for c in range(3):
                edge_bonds[c, i] = bonds[c]
        if add:
            totals = [totals[0] + density[4], totals[1] + bond[4]]
        density[4], bond[4] = totals
        return totals[0]

    def edge_pulls(value):
        totals = [nothing(8, 128)] * 3
        for i, dz in enumerate(ZS):
            own = pltpu.roll(value, dz % 128, 1) if dz else value
            here = [nothing(8, 128)] * 3
            for a, b in BY_Z[dz]:
                both = own + slope_of(4, a, b)
                for c in range(3):
                    here[c] = here[c] + both * weighted[c, ORDER[a, b, dz], 4]
            for c in range(3):
                totals[c] = totals[c] + home(PULL_BOND * edge_bonds[c, i] + PULL_DENS * here[c], dz)
        for c in range(3):
            pull[c, 4] = totals[c]

    def slope_pulls(k, wanted):
        totals = [nothing(8, 128)] * 3
        for dz in ZS:
            here = [nothing(8, 128)] * 3
            for a, b in BY_Z[dz]:
                if not wanted(a):
                    continue
                s = slope_of(k, a, b)
                for c in range(3):
                    here[c] = here[c] + s * weighted[c, ORDER[a, b, dz], k]
            totals = [x + home(y, dz) for x, y in zip(totals, here)]
        return totals

    def keep(k, totals, value):
        density[k] = totals[0]
        bond[k] = totals[1]
        for c in range(3):
            pull[c, k] = PULL_BOND * totals[2 + c] + PULL_DENS * (value * totals[5 + c])

    def add_pulls(k, totals):
        for c in range(3):
            pull[c, k] = pull[c, k] + PULL_DENS * totals[c]

    every, behind, beyond = (lambda a: True), (lambda a: a <= 0), (lambda a: a > 0)
    both_ways = (-3, -2, -1, 1, 2, 3)

    def loop(first, last, act):
        def run(k, carry):
            act(k)
            return carry

        lax.fori_loop(first, last, run, 0)

    slope[...] = nothing(6, 16, 128)
    slope_moved[...] = nothing(7, 6, 16, 128)
    loop(0, 6, take_tile)
    pl.when(ahead & least)(far)
    loop(0, 4, lambda k: move_tile(k, both_ways))
    move_tile(4, (-3, -2, -1))
    roll_slope(0, slope_value(0, ghost_density(0)))

    def own_whole(k):
        totals = own_pairs(k)
        value = slope_value(k, totals[0])
        keep(k, totals, value)
        roll_slope(k, value)

    loop(1, 4, own_whole)
    pl.when(ahead & ~least & ~most)(far)
    loop(1, 3, lambda k: move_slope(k, both_ways))
    move_slope(3, (-3, -2, -1))
    loop(1, 3, lambda k: add_pulls(k, slope_pulls(k, every)))
    add_pulls(3, slope_pulls(3, behind))
    for i, dz in enumerate(ZS):
        v = centre_of(4, dz)
        for c in range(3):
            centres[c, i] = v[c]

    edge_pairs(behind, False)

    pl.when(ahead & most)(far)
    all_sent()
    far_got()

    for k in (6, 7):
        take_tile(k, far_occ.at[jnp.where(ahead, k - 6, 7 - k)])
    move_tile(4, (1, 2, 3))
    move_tile(5, both_ways)
    value = slope_value(4, edge_pairs(beyond, True))
    roll_slope(4, value)
    roll_slope(5, slope_value(5, ghost_density(5)))
    move_slope(4, both_ways)
    edge_pulls(value)
    move_slope(3, (1, 2, 3))
    add_pulls(3, slope_pulls(3, beyond))

    first_part, back, back_rows, back_slots = back_indices()

    def native(at):
        v = [at(place(p, 4) + 1) for p in range(4)]
        v = [pick(x, back, 1) for x in v]
        v = [jnp.where(first_part, v[2 * h], v[2 * h + 1]) for h in range(2)]
        v = [pick(x, back_rows, 0) for x in v]
        return pick(jnp.where(row < 4, v[0], v[1]), back_slots, 1)

    def store(dst, v):
        for t in range(4):
            dst[t, 0] = jnp.where(occ_v[t] != 0, v[2 * t : 2 * t + 2], 0.0)

    for c in range(3):
        store(force_ref.at[c], native(lambda k: pull[c, k]))

    def energy_of(k):
        d = density[k] * DENS_SCALE
        return BOND_SCALE * bond[k] - jnp.sqrt(d + 0.5) + 0.002 * d * d

    store(energy_ref, native(energy_of))


def put_out(force_in, energy_in, force_ref, energy_ref, sems):
    copies = [
        pltpu.make_async_copy(force_in, force_ref, sems.at[0]),
        pltpu.make_async_copy(energy_in, energy_ref, sems.at[1]),
    ]
    for x in copies:
        x.start()
    for x in copies:
        x.wait()


def scratch():
    f32 = lambda *s: pltpu.VMEM(s, jnp.float32)
    return [
        f32(3, 8, 16, 128),
        pltpu.VMEM((4, 2, 128), jnp.int32),
        pltpu.VMEM((2, 16, 128), jnp.int32),
        f32(3, 4, 8, 16, 128),
        f32(3, 7, 6, 16, 128),
        f32(3, len(ZS), 8, 128),
        f32(6, 16, 128),
        f32(4, 6, 8, 128),
        f32(7, 6, 16, 128),
        f32(6, 8, 128),
        f32(6, 8, 128),
        f32(3, 6, 8, 128),
        f32(3, len(ZS), 8, 128),
        f32(3, len(VECTORS), 6, 8, 128),
        f32(192, 128),
        pltpu.SemaphoreType.DMA((2,)),
        pltpu.SemaphoreType.DMA((2,)),
        pltpu.SemaphoreType.DMA((2,)),
        pltpu.SemaphoreType.REGULAR,
    ]


def solution(mesh):
    sizes = tuple(mesh.shape[a] for a in ("gx", "gy", "gz"))

    def step(positions, occupied):
        positions, occupied = (pltpu.with_memory_space_constraint(x, pltpu.HBM) for x in (positions, occupied))
        found = pl.pallas_call(
            lambda *refs: atoms(sizes, *refs),
            out_shape=(pltpu.VMEM((3, 4, 1, 2, 128), jnp.float32), pltpu.VMEM((4, 1, 2, 128), jnp.float32)),
            in_specs=[pl.BlockSpec(memory_space=pl.ANY)] * 2,
            out_specs=[pl.BlockSpec(memory_space=pltpu.VMEM)] * 2,
            scratch_shapes=scratch(),
            compiler_params=pltpu.CompilerParams(
                collective_id=0, has_side_effects=True, vmem_limit_bytes=40 * 2**20
            ),
        )(positions, occupied)
        found = [pltpu.with_memory_space_constraint(x, pltpu.VMEM) for x in found]
        return pl.pallas_call(
            put_out,
            out_shape=[jax.ShapeDtypeStruct(x.shape, x.dtype) for x in found],
            in_specs=[pl.BlockSpec(memory_space=pltpu.VMEM)] * 2,
            out_specs=[pl.BlockSpec(memory_space=pl.ANY)] * 2,
            scratch_shapes=[pltpu.SemaphoreType.DMA((2,))],
        )(*found)

    in_specs = (P(None, "gx", "gy", "gz", None), P("gx", "gy", "gz", None))
    out_specs = (P(None, "gx", "gy", "gz", None), P("gx", "gy", "gz", None))
    return jax.shard_map(step, mesh=mesh, in_specs=in_specs, out_specs=out_specs, check_vma=False)
```

```python
import math

import jax
import jax.numpy as jnp
from jax import lax
from jax.experimental import pallas as pl
from jax.experimental.pallas import tpu as pltpu
from jax.sharding import PartitionSpec as P

MESH = pl.DeviceIdType.MESH

lattice_step = 3.615
cut_radius = 4.9
far_away = 1000.0

TILE_X = 2 * lattice_step
TILE_YZ = 4 * lattice_step
REACH = 3


def displacements():
    found = []
    near = lambda n: max(0.0, abs(n) * 0.5 * lattice_step - 0.7) ** 2
    for a in range(-4, 5):
        for b in range(-4, 5):
            for c in range(-4, 5):
                if (a + b + c) % 2 == 0 and (a, b, c) != (0, 0, 0):
                    if near(a) + near(b) + near(c) < cut_radius * cut_radius + 0.01:
                        found.append((a, b, c))
    return found


VECTORS = displacements()
ZS = sorted({v[2] for v in VECTORS})
BY_Z = {dz: [(v[0], v[1]) for v in VECTORS if v[2] == dz] for dz in ZS}
ORDER = {v: i for i, v in enumerate([(a, b, dz) for dz in ZS for a, b in BY_Z[dz]])}

LOG2E = 1.0 / math.log(2.0)
DECAY = 5.85 / 2.556
MORSE = 1.36
K_DENS = -DECAY * cut_radius * LOG2E
DENS_SCALE = math.exp(5.85)
K_BOND = -MORSE * cut_radius * LOG2E
C_BOND = MORSE * 2.556 * LOG2E
FOUR = 4.0 / cut_radius
BOND_SCALE = 0.5 * 0.3
PULL_BOND = -0.3 * 2.0 * MORSE
PULL_DENS = -DECAY * DENS_SCALE


def iotas():
    return (
        lax.broadcasted_iota(jnp.int32, (8, 128), 0),
        lax.broadcasted_iota(jnp.int32, (8, 128), 1),
    )


def pick(x, idx, axis):
    return jnp.take_along_axis(x, idx, axis=axis, mode="promise_in_bounds")


def turn_indices():
    row, lane = iotas()
    quarter, rest = lane // 32, lane % 32
    xs, zs = rest // 8, rest % 8
    y = (quarter - row % 4 + 4) % 4
    basis = jnp.where(xs % 2 == 0, 3 * (zs % 2), 1 + zs % 2)
    first = (xs // 2) * 64 + y * 16 + (zs // 2) * 4 + basis
    second = (row // 4) * 4 + (quarter - row % 4 + 4) % 4
    return first, second


def back_indices():
    row, lane = iotas()
    quarter, rest = lane // 32, lane % 32
    part = (quarter - row + 10) % 4
    first = (rest // 8) * 32 + (part % 2 + 1) * 8 + lane % 8
    second = 2 + (quarter - row % 4 + 4) % 4
    basis = lane % 4
    xs = 2 * (lane // 64) + jnp.where((basis == 1) | (basis == 2), 1, 0)
    zs = 2 * ((lane // 4) % 4) + basis // 2
    third = (((lane // 16) % 4 + row) % 4) * 32 + xs * 8 + zs
    return part < 2, first, second, third


YZ = sorted(((b, c) for b in (-1, 0, 1) for c in (-1, 0, 1)), key=lambda v: -abs(v[0]) - abs(v[1]))


def exchange(sizes, pos_ref, occ_ref, raw_ref, far_occ, counted, send, recv, near_go):
    n_x, n_y, n_z = sizes
    me_x, me_y, me_z = (lax.axis_index(a) for a in ("gx", "gy", "gz"))
    inner = (me_x == 1) | (me_x == 2)
    low_pair = me_x < 2
    my_outer = jnp.where(low_pair, 0, 3)
    mate = jnp.where(low_pair, 1 - me_x, 5 - me_x)
    barrier = pltpu.get_barrier_semaphore()

    def there(b, c, sign=1):
        ok = []
        for step, me, n in ((b * sign, me_y, n_y), (c * sign, me_z, n_z)):
            if step == 1:
                ok.append(me < n - 1)
            if step == -1:
                ok.append(me > 0)
        return ok

    def when(conditions, act):
        if not conditions:
            return act()
        both = conditions[0]
        for x in conditions[1:]:
            both = both & x
        pl.when(both)(act)

    def count(steps):
        total = 0
        for b, c in steps:
            ok = there(b, c)
            if not ok:
                total = total + 1
                continue
            both = ok[0]
            for x in ok[1:]:
                both = both & x
            total = total + both.astype(jnp.int32)
        return total

    def greet(x, b, c):
        pl.semaphore_signal(
            barrier, inc=1, device_id=(x, me_y + b, me_z + c), device_id_type=MESH
        )

    around = [v for v in YZ if v != (0, 0)]

    def enter():
        def as_inner():
            for b, c in YZ:
                when(there(b, c), lambda b=b, c=c: greet(3 - me_x, b, c))
            greet(mate, 0, 0)

        pl.when(inner)(as_inner)
        for b, c in around:
            when(there(b, c), lambda b=b, c=c: greet(my_outer, b, c))

    def copies(v, part):
        a, b, c = v
        x_from, x_to, x_n = {0: (0, 2, 4), 1: (2, 0, 2), -1: (0, 6, 2)}[a]
        z_from, z_to, z_n = {0: (0, 1, 2), 1: (1, 0, 1), -1: (0, 3, 1)}[c]
        row = 4 * (1 - b) + z_to

        def remote(src, dst):
            return pltpu.make_async_remote_copy(
                src_ref=src,
                dst_ref=dst,
                send_sem=send.at[part],
                recv_sem=recv.at[part],
                device_id=(me_x + a, me_y + b, me_z + c),
                device_id_type=MESH,
            )

        dst = raw_ref.at[:, x_to : x_to + x_n, row : row + z_n]
        if part == 0:
            return [remote(raw_ref.at[:, 2 + x_from : 2 + x_from + x_n, 5 + z_from : 5 + z_from + z_n], dst)]
        at = (slice(x_from, x_from + x_n), 0, slice(z_from, z_from + z_n))
        return [
            remote(pos_ref.at[(slice(None), *at)], dst),
            remote(occ_ref.at[at], far_occ.at[:, row : row + z_n]),
        ]

    def start(a, part):
        for b, c in YZ:
            if (a, b, c) != (0, 0, 0):

                def run(v=(a, b, c)):
                    for x in copies(v, part):
                        x.start()

                when(there(b, c), run)

    even = lax.rem(me_x, 2) == 0
    end_y, end_z = (me_y == 0) | (me_y == n_y - 1), (me_z == 0) | (me_z == n_z - 1)

    def wait(sem, each, less=0):
        for last_y in (False, True):
            for last_z in (False, True):
                rows = each * (2 if last_y else 3) * (3 if last_z else 4) - less

                def run(rows=rows):
                    ref = counted.at[0:rows]
                    pltpu.make_async_copy(ref, ref, sem).wait()

                pl.when((end_y == last_y) & (end_z == last_z))(run)

    def far_inner():
        pl.semaphore_wait(barrier, count(YZ))
        pl.when(me_x == 1)(lambda: start(1, 1))
        pl.when(me_x == 2)(lambda: start(-1, 1))

    def far():
        pl.when(inner)(far_inner)

    def near_outer():
        pl.semaphore_wait(barrier, count(around) + count(YZ))
        pl.semaphore_signal(near_go, inc=1, device_id=(mate, me_y, me_z), device_id_type=MESH)

    def near():
        pl.when(~inner)(near_outer)
        pl.when(inner)(lambda: pl.semaphore_wait(near_go, 1))
        start(0, 0)
        pl.when(even)(lambda: start(1, 0))
        pl.when(~even)(lambda: start(-1, 0))

    def near_got():
        wait(recv.at[0], 18, 24)

    def far_got():
        pl.when(inner)(lambda: wait(recv.at[1], 8))

    def near_sent():
        wait(send.at[0], 18, 24)

    def far_sent():
        pl.when(inner)(lambda: wait(send.at[1], 8))

    return enter, near, far, near_got, far_got, near_sent, far_sent


def pair_density(centre, near):
    sep = [n - c for n, c in zip(near, centre)]
    dist_sq = sep[0] * sep[0] + sep[1] * sep[1] + sep[2] * sep[2]
    inside = jnp.maximum(1.0 - dist_sq, 0.0)
    inverse = lax.rsqrt(dist_sq)
    radius = dist_sq * inverse
    part = jnp.exp2(K_DENS * radius) * inside
    return sep, inside, inverse, radius, part


def pair_all(centre, near):
    sep, inside, inverse, radius, part = pair_density(centre, near)
    nearer = jnp.exp2(K_BOND * radius + C_BOND)
    less = nearer - 2.0
    near_in = nearer * inside
    over = inside * inverse
    pull_bond = near_in * ((nearer - 1.0) * over + (FOUR / (2.0 * MORSE)) * less)
    pull_dens = part * (over + FOUR / DECAY)
    return sep, part * inside, near_in * inside * less, pull_bond, pull_dens


def atoms(sizes, pos_ref, occ_ref, force_ref, energy_ref, raw, occ_v, far_occ, rolled, moved, centres, slope, slope_rolled, slope_moved, density, bond, pull, edge_bonds, weighted, counted, local, send, recv, near_go):
    n_x, n_y, n_z = sizes
    me_x, me_y, me_z = (lax.axis_index(a) for a in ("gx", "gy", "gz"))
    enter, near, far, near_got, far_got, near_sent, far_sent = exchange(sizes, pos_ref, occ_ref, raw, far_occ, counted, send, recv, near_go)
    get_pos = pltpu.make_async_copy(pos_ref.at[:, :, 0], raw.at[:, 2:6, 5:7], local.at[0])
    get_occ = pltpu.make_async_copy(occ_ref.at[:, 0], occ_v, local.at[1])
    far_occ[...] = jnp.ones((2, 16, 128), jnp.int32)
    get_pos.start()
    get_occ.start()

    def load():
        get_occ.wait()
        get_pos.wait()
        for t in range(4):
            empty = jnp.where(occ_v[t] != 0, 0.0, far_away)
            raw[0, 2 + t, 5:7] = raw[0, 2 + t, 5:7] + empty

    ahead = me_x < 2
    most = me_y < n_y // 2
    least = me_y >= (5 * n_y) // 8
    at_once = (me_x == 2) & most

    def send_first():
        far()
        enter()
        load()

    def greet_first():
        enter()
        load()

    pl.when(at_once)(send_first)
    pl.when(~at_once)(greet_first)
    pl.when(~ahead & ~most)(far)
    near()

    nothing = lambda *s: jnp.zeros(s, jnp.float32)

    def blank_x(t):
        def run():
            raw[:, t : t + 2] = nothing(3, 2, 16, 128)

        return run

    def blank_rows(rows):
        def run():
            for r in rows:
                raw[:, :, r : r + 1] = nothing(3, 8, 1, 128)

        return run

    pl.when(me_x == 0)(blank_x(0))
    pl.when(me_x == n_x - 1)(blank_x(6))
    pl.when(me_y == 0)(blank_rows((0, 1, 2, 3)))
    pl.when(me_y == n_y - 1)(blank_rows((8, 9, 10, 11)))
    pl.when(me_z == 0)(blank_rows((0, 4, 8)))
    pl.when(me_z == n_z - 1)(blank_rows((3, 7, 11)))

    row, lane = iotas()
    turn = turn_indices()
    third = (lane % 32) // 8
    quarter = lane // 32
    out_z = ((me_z == 0) & (third == 0)) | ((me_z == n_z - 1) & (third == 3))
    far_z = jnp.where(out_z, far_away, 0.0)
    shift_z = (third - 1).astype(jnp.float32) * TILE_YZ
    odds = [(quarter + lane + a) % 2 == 1 for a in (0, 1)]
    unit = 1.0 / cut_radius

    reach = jnp.where(ahead, quarter, 3 - quarter)

    def place(k, n):
        return jnp.where(ahead, k, n - 1 - k)

    planes = [((third + row) % 4) * 32 + ((quarter + jnp.where(ahead, a, 4 - a)) % 4) * 8 + lane % 8 for a in range(4)]

    near_got()

    def take_tile(k, occupied=None):
        t = place(k, 8)
        out_x = ((me_x == 0) & (t < 2)) | ((me_x == n_x - 1) & (t > 5))
        far_x = jnp.where(out_x, far_away, 0.0) + (t - 2).astype(jnp.float32) * TILE_X
        for half in range(2):
            rows = slice(8 * half, 8 * half + 8)
            tile_y = 2 * half + row // 4
            out_y = ((me_y == 0) & (tile_y == 0)) | ((me_y == n_y - 1) & (tile_y == 2))
            shifts = [
                far_z + jnp.where(out_y, far_away, 0.0) + far_x,
                (tile_y - 1).astype(jnp.float32) * TILE_YZ,
                shift_z,
            ]
            for c in range(3):
                v = raw[c, t, rows]
                if c == 0 and occupied is not None:
                    v = v + jnp.where(occupied[rows] != 0, 0.0, far_away)
                v = pick(pick(v, turn[0], 1), turn[1], 0)
                for a in range(4):
                    rolled[c, a, k, rows] = (pick(v, planes[a], 1) + shifts[c]) * unit

    def roll_planes(v, put):
        back, half, on = (pltpu.roll(v, 32 * m, 1) for m in (1, 2, 3))
        put(1)[...] = jnp.where(ahead, on, back)
        put(2)[...] = half
        put(3)[...] = jnp.where(ahead, back, on)

    def crossing(a):
        return reach + a > 3 if a > 0 else reach + a < 0

    def move_tile(k, shifts):
        for a in shifts:
            for c in range(3):
                for half in range(2):
                    rows = slice(8 * half, 8 * half + 8)
                    other = k + 2 if a > 0 else k
                    moved[c, a + 3, k, rows] = jnp.where(
                        crossing(a), rolled[c, a % 4, other, rows], rolled[c, a % 4, k + 1, rows]
                    )

    def roll_slope(k, value):
        slope[k, 2:10] = value
        roll_planes(value, lambda a: slope_rolled.at[a, k])

    def move_slope(k, shifts):
        for a in shifts:
            other = k + 1 if a > 0 else k - 1
            slope_moved[a + 3, k, 2:10] = jnp.where(
                crossing(a), slope_rolled[a % 4, other], slope_rolled[a % 4, k]
            )

    def rows_of(get, a, b):
        if b % 2 == 0:
            r = 2 + b // 2
            return [x[r : r + 8] for x in get]
        r = 2 + (b + 1) // 2
        return [jnp.where(odds[a % 2], x[r - 1 : r + 7], x[r : r + 8]) for x in get]

    def near_of(k, a, b):
        return rows_of([moved.at[c, a + 3, k] if a else rolled.at[c, 0, k + 1] for c in range(3)], a, b)

    def slope_of(k, a, b):
        return rows_of([slope_moved.at[a + 3, k] if a else slope.at[k]], a, b)[0]

    def centre_of(k, dz):
        return [pltpu.roll(rolled[c, 0, k + 1, 2:10], dz % 128, 1) if dz else rolled[c, 0, k + 1, 2:10] for c in range(3)]

    def home(x, dz):
        return pltpu.roll(x, (-dz) % 128, 1) if dz else x

    def slope_value(k, total):
        total = total * DENS_SCALE
        value = -0.5 * lax.rsqrt(total + 0.5) + 0.004 * total
        return jnp.where(rolled[0, 0, k + 1, 2:10] < 0.5 * far_away / cut_radius, value, 0.0)

    def ghost_density(k):
        total = nothing(8, 128)
        for dz in ZS:
            centre = centre_of(k, dz)
            here = nothing(8, 128)
            for a, b in BY_Z[dz]:
                _, inside, _, _, part = pair_density(centre, near_of(k, a, b))
                here = here + part * inside
            total = total + home(here, dz)
        return total

    def own_pairs(k):
        totals = [nothing(8, 128)] * 8
        for dz in ZS:
            centre = centre_of(k, dz)
            here = [nothing(8, 128)] * 8
            for a, b in BY_Z[dz]:
                sep, dens, bonding, pull_bond, pull_dens = pair_all(centre, near_of(k, a, b))
                here[0] = here[0] + dens
                here[1] = here[1] + bonding
                for c in range(3):
                    here[2 + c] = here[2 + c] + pull_bond * sep[c]
                    w = pull_dens * sep[c]
                    here[5 + c] = here[5 + c] + w
                    weighted[c, ORDER[a, b, dz], k] = w
            totals = [x + home(y, dz) for x, y in zip(totals, here)]
        return totals

    def edge_pairs(wanted, add):
        totals = [nothing(8, 128)] * 2
        for i, dz in enumerate(ZS):
            centre = [centres[c, i] for c in range(3)]
            here = [nothing(8, 128)] * 2
            bonds = [edge_bonds[c, i] if add else nothing(8, 128) for c in range(3)]
            for a, b in BY_Z[dz]:
                if not wanted(a):
                    continue
                sep, dens, bonding, pull_bond, pull_dens = pair_all(centre, near_of(4, a, b))
                here = [here[0] + dens, here[1] + bonding]
                for c in range(3):
                    bonds[c] = bonds[c] + pull_bond * sep[c]
                    weighted[c, ORDER[a, b, dz], 4] = pull_dens * sep[c]
            totals = [x + home(y, dz) for x, y in zip(totals, here)]
            for c in range(3):
                edge_bonds[c, i] = bonds[c]
        if add:
            totals = [totals[0] + density[4], totals[1] + bond[4]]
        density[4], bond[4] = totals
        return totals[0]

    def edge_pulls(value):
        totals = [nothing(8, 128)] * 3
        for i, dz in enumerate(ZS):
            own = pltpu.roll(value, dz % 128, 1) if dz else value
            here = [nothing(8, 128)] * 3
            for a, b in BY_Z[dz]:
                both = own + slope_of(4, a, b)
                for c in range(3):
                    here[c] = here[c] + both * weighted[c, ORDER[a, b, dz], 4]
            for c in range(3):
                totals[c] = totals[c] + home(PULL_BOND * edge_bonds[c, i] + PULL_DENS * here[c], dz)
        for c in range(3):
            pull[c, 4] = totals[c]

    def slope_pulls(k, wanted):
        totals = [nothing(8, 128)] * 3
        for dz in ZS:
            here = [nothing(8, 128)] * 3
            for a, b in BY_Z[dz]:
                if not wanted(a):
                    continue
                s = slope_of(k, a, b)
                for c in range(3):
                    here[c] = here[c] + s * weighted[c, ORDER[a, b, dz], k]
            totals = [x + home(y, dz) for x, y in zip(totals, here)]
        return totals

    def keep(k, totals, value):
        density[k] = totals[0]
        bond[k] = totals[1]
        for c in range(3):
            pull[c, k] = PULL_BOND * totals[2 + c] + PULL_DENS * (value * totals[5 + c])

    def add_pulls(k, totals):
        for c in range(3):
            pull[c, k] = pull[c, k] + PULL_DENS * totals[c]

    every, behind, beyond = (lambda a: True), (lambda a: a <= 0), (lambda a: a > 0)
    both_ways = (-3, -2, -1, 1, 2, 3)

    def loop(first, last, act):
        def run(k, carry):
            act(k)
            return carry

        lax.fori_loop(first, last, run, 0)

    slope[...] = nothing(6, 16, 128)
    slope_moved[...] = nothing(7, 6, 16, 128)
    loop(0, 6, take_tile)
    pl.when(ahead & least)(far)
    loop(0, 4, lambda k: move_tile(k, both_ways))
    move_tile(4, (-3, -2, -1))
    roll_slope(0, slope_value(0, ghost_density(0)))

    def own_whole(k):
        totals = own_pairs(k)
        value = slope_value(k, totals[0])
        keep(k, totals, value)
        roll_slope(k, value)

    loop(1, 4, own_whole)
    pl.when(ahead & ~least & ~most)(far)
    loop(1, 3, lambda k: move_slope(k, both_ways))
    move_slope(3, (-3, -2, -1))
    loop(1, 3, lambda k: add_pulls(k, slope_pulls(k, every)))
    add_pulls(3, slope_pulls(3, behind))
    for i, dz in enumerate(ZS):
        v = centre_of(4, dz)
        for c in range(3):
            centres[c, i] = v[c]

    edge_pairs(behind, False)

    near_sent()
    pl.when(ahead & most)(far)
    far_got()

    for k in (6, 7):
        take_tile(k, far_occ.at[jnp.where(ahead, k - 6, 7 - k)])
    move_tile(4, (1, 2, 3))
    move_tile(5, both_ways)
    value = slope_value(4, edge_pairs(beyond, True))
    roll_slope(4, value)
    roll_slope(5, slope_value(5, ghost_density(5)))
    move_slope(4, both_ways)
    edge_pulls(value)
    move_slope(3, (1, 2, 3))
    add_pulls(3, slope_pulls(3, beyond))

    first_part, back, back_rows, back_slots = back_indices()

    def native(at):
        v = [at(place(p, 4) + 1) for p in range(4)]
        v = [pick(x, back, 1) for x in v]
        v = [jnp.where(first_part, v[2 * h], v[2 * h + 1]) for h in range(2)]
        v = [pick(x, back_rows, 0) for x in v]
        return pick(jnp.where(row < 4, v[0], v[1]), back_slots, 1)

    def store(dst, v):
        for t in range(4):
            dst[t, 0] = jnp.where(occ_v[t] != 0, v[2 * t : 2 * t + 2], 0.0)

    for c in range(3):
        store(force_ref.at[c], native(lambda k: pull[c, k]))

    def energy_of(k):
        d = density[k] * DENS_SCALE
        return BOND_SCALE * bond[k] - jnp.sqrt(d + 0.5) + 0.002 * d * d

    store(energy_ref, native(energy_of))
    far_sent()


def put_out(force_in, energy_in, force_ref, energy_ref, sems):
    copies = [
        pltpu.make_async_copy(force_in, force_ref, sems.at[0]),
        pltpu.make_async_copy(energy_in, energy_ref, sems.at[1]),
    ]
    for x in copies:
        x.start()
    for x in copies:
        x.wait()


def scratch():
    f32 = lambda *s: pltpu.VMEM(s, jnp.float32)
    return [
        f32(3, 8, 16, 128),
        pltpu.VMEM((4, 2, 128), jnp.int32),
        pltpu.VMEM((2, 16, 128), jnp.int32),
        f32(3, 4, 8, 16, 128),
        f32(3, 7, 6, 16, 128),
        f32(3, len(ZS), 8, 128),
        f32(6, 16, 128),
        f32(4, 6, 8, 128),
        f32(7, 6, 16, 128),
        f32(6, 8, 128),
        f32(6, 8, 128),
        f32(3, 6, 8, 128),
        f32(3, len(ZS), 8, 128),
        f32(3, len(VECTORS), 6, 8, 128),
        f32(192, 128),
        pltpu.SemaphoreType.DMA((2,)),
        pltpu.SemaphoreType.DMA((2,)),
        pltpu.SemaphoreType.DMA((2,)),
        pltpu.SemaphoreType.REGULAR,
    ]


def solution(mesh):
    sizes = tuple(mesh.shape[a] for a in ("gx", "gy", "gz"))

    def step(positions, occupied):
        positions, occupied = (pltpu.with_memory_space_constraint(x, pltpu.HBM) for x in (positions, occupied))
        found = pl.pallas_call(
            lambda *refs: atoms(sizes, *refs),
            out_shape=(pltpu.VMEM((3, 4, 1, 2, 128), jnp.float32), pltpu.VMEM((4, 1, 2, 128), jnp.float32)),
            in_specs=[pl.BlockSpec(memory_space=pl.ANY)] * 2,
            out_specs=[pl.BlockSpec(memory_space=pltpu.VMEM)] * 2,
            scratch_shapes=scratch(),
            compiler_params=pltpu.CompilerParams(
                collective_id=0, has_side_effects=True, vmem_limit_bytes=40 * 2**20
            ),
        )(positions, occupied)
        found = [pltpu.with_memory_space_constraint(x, pltpu.VMEM) for x in found]
        return pl.pallas_call(
            put_out,
            out_shape=[jax.ShapeDtypeStruct(x.shape, x.dtype) for x in found],
            in_specs=[pl.BlockSpec(memory_space=pltpu.VMEM)] * 2,
            out_specs=[pl.BlockSpec(memory_space=pl.ANY)] * 2,
            scratch_shapes=[pltpu.SemaphoreType.DMA((2,))],
        )(*found)

    in_specs = (P(None, "gx", "gy", "gz", None), P("gx", "gy", "gz", None))
    out_specs = (P(None, "gx", "gy", "gz", None), P("gx", "gy", "gz", None))
    return jax.shard_map(step, mesh=mesh, in_specs=in_specs, out_specs=out_specs, check_vma=False)
```
